512 devices in a mesh: section: 16 (over z, core), tm: 32 (over x, y).
Axes of the slice: x: 4, y: 8, z: 8, core: 2. Of those that a mesh axis runs over, the one named last changes fastest.
Arguments:
- acts_in: bfloat16 [16, 4096, 2048], P('section', 'tm'), may hold values from -6 to 6
- saved_in: bfloat16 [16, 4096, 2048], P('section', 'tm'), may hold values from -6 to 6
- grad_in: bfloat16 [16, 4096, 2048], P('section', 'tm'), may hold values from -6 to 6
- gate_a: bfloat16 [16, 2, 8, 256, 256], P('section', None, None, 'tm'), may hold values from -0.375 to 0.375
- gate_x: bfloat16 [16, 2, 8, 256, 256], P('section', None, None, 'tm'), may hold values from -0.375 to 0.375
- bias_a: float32 [16, 2, 2048], P('section'), may hold values from -4 to 4
- bias_x: float32 [16, 2, 2048], P('section'), may hold values from -4 to 4
- rate_param: float32 [16, 2, 2048], P('section'), may hold values from -16 to -3.5, as said below
- norm_gain: float32 [16, 2, 2048], P('section'), may hold values from 0.5 to 1.5
- section_layers: int32 [16], P('section'), may hold values from 1 to 2
Outputs:
- acts_out: bfloat16 [16, 4096, 2048], P('section', 'tm')
- grad_out: bfloat16 [16, 4096, 2048], P('section', 'tm')
- grad_gain: float32 [16, 2, 2048], P('section')
- grad_bias_a: float32 [16, 2, 2048], P('section')
- grad_bias_x: float32 [16, 2, 2048], P('section')
- grad_rate: float32 [16, 2, 2048], P('section')
The draws below stay inside these ranges and needn't reach their ends.
Inputs may be any that keep to these rules, and one draw needn't show every extreme that they name: `rate_param`: softplus of every entry lies between 0.05 / 4096 and 0.02.
All inputs are finite; a program needn't handle non-finite values.
Results may differ from the reference program's by a relative error of at most 0.015.
Values may be sent and summed in bfloat16 or wider, within the bound.
A program may use at most 192 MiB of HBM per device.

```python
import math
import jax
import jax.numpy as jnp
from jax import lax

HEADS = 8
HW = 256
LSLOT = 2
C = 2048
SEQ = 4096
SECTIONS = 16


def draw_rate_param(key, part):
    base = jax.random.fold_in(key, 11)
    key_pick, key_slow, key_quick = jax.random.split(base, 3)
    shape = (SECTIONS, LSLOT, C)
    quick_share = 0.5
    picked = jax.random.uniform(key_pick, shape, dtype=jnp.float32) < quick_share
    slow_rate = jnp.exp(jax.random.uniform(key_slow, shape, dtype=jnp.float32, minval=math.log(0.05 / SEQ), maxval=math.log(0.2 / SEQ)))
    quick_rate = jnp.exp(jax.random.uniform(key_quick, shape, dtype=jnp.float32, minval=math.log(0.004), maxval=math.log(0.02)))
    decay_rate = jnp.where(picked, quick_rate, slow_rate)
    return jnp.log(jnp.expm1(decay_rate)).astype(jnp.float32)


def set_ends(drawn, stream_key, low, top_value):
    dims = drawn.shape
    index_at = [jax.random.randint(jax.random.fold_in(stream_key, axis), (), 0, dims[axis]) for axis in range(len(dims))]
    drawn = drawn.at[tuple(index_at)].set(low)
    longest = dims.index(max(dims))
    index_at[longest] = (index_at[longest] + 1) % dims[longest]
    return drawn.at[tuple(index_at)].set(top_value)


def levels(own_key, shape, pieces, low, high):
    factor_of, own = 1.0, jax.random.fold_in(own_key, 6)
    for axis_at, blocks in pieces:
        draws = jnp.exp(jax.random.uniform(jax.random.fold_in(own, axis_at), (blocks,), jnp.float32, low / len(pieces), high / len(pieces)))
        factor_of = factor_of * jnp.repeat(draws, shape[axis_at] // blocks).reshape([-1 if axis == axis_at else 1 for axis in range(len(shape))])
    return factor_of


def normal_values(stream_key, dims, scale, most, shards=(), kind=jnp.bfloat16):
    values = scale * jax.random.normal(stream_key, dims, jnp.float32)
    if shards:
        values = values * levels(stream_key, dims, shards, -0.22, 0.18)
    return jnp.clip(values, -most, most).astype(kind)


def setup_inputs(seed: int = 0) -> dict:
    streams_of = jax.random.split(jax.random.key(seed), 11)
    return {
        "acts_in": normal_values(streams_of[0], (SECTIONS, SEQ, C), 1.0, 6.0, ((0, 16), (1, 32))),
        "saved_in": normal_values(streams_of[1], (SECTIONS, SEQ, C), 1.0, 6.0, ((0, 16), (1, 32))),
        "grad_in": normal_values(streams_of[2], (SECTIONS, SEQ, C), 1.0, 6.0, ((0, 16), (1, 32))),
        "gate_a": normal_values(streams_of[3], (SECTIONS, LSLOT, HEADS, HW, HW), HW ** -0.5, 0.375, ((0, 16), (3, 32))),
        "gate_x": normal_values(streams_of[4], (SECTIONS, LSLOT, HEADS, HW, HW), HW ** -0.5, 0.375, ((0, 16), (3, 32))),
        "bias_a": normal_values(streams_of[5], (SECTIONS, LSLOT, C), 1.0, 4.0, ((0, 16),), jnp.float32),
        "bias_x": normal_values(streams_of[6], (SECTIONS, LSLOT, C), 1.0, 4.0, ((0, 16),), jnp.float32),
        "rate_param": draw_rate_param(jax.random.fold_in(streams_of[10], 71), 0),
        "norm_gain": jnp.clip(1.0 + 0.1 * jax.random.normal(streams_of[8], (SECTIONS, LSLOT, C), jnp.float32), 0.5, 1.5),
        "section_layers": set_ends(jax.random.randint(streams_of[9], (SECTIONS,), 1, LSLOT + 1), jax.random.fold_in(streams_of[9], 1), 1, LSLOT).astype(jnp.int32),
    }


EPS = 1e-06

def combine(earlier, later):
    return (earlier[0] * later[0], later[0] * earlier[1] + later[1])

def blockdiag(inputs, weight):
    rows_all = inputs.shape[0]
    inputs3 = inputs.astype(jnp.float32).reshape(rows_all, HEADS, HW)
    result = jnp.einsum('thi,hio->tho', inputs3, weight.astype(jnp.float32))
    return result.reshape(rows_all, HEADS * HW)

def blockdiag_t(grads, weight):
    rows_all = grads.shape[0]
    grads3 = grads.astype(jnp.float32).reshape(rows_all, HEADS, HW)
    result = jnp.einsum('tho,hio->thi', grads3, weight.astype(jnp.float32))
    return result.reshape(rows_all, HEADS * HW)

def layer_forward(x_in, w_a, w_x, b_a, b_x, rate_p, gain, live_mask):
    x_float = x_in.astype(jnp.float32)
    mean_sq = lax.optimization_barrier(jnp.mean(x_float * x_float, axis=-1, keepdims=True))
    inv_rms = lax.rsqrt(mean_sq + EPS)
    normed = x_float * inv_rms
    normed_in = (normed * gain).astype(jnp.bfloat16)
    u_float = normed_in.astype(jnp.float32)
    pre_a = blockdiag(normed_in, w_a) + b_a
    pre_x = blockdiag(normed_in, w_x) + b_x
    reset_gate = jax.nn.sigmoid(pre_a)
    input_gate = jax.nn.sigmoid(pre_x)
    decay_rate = jax.nn.softplus(rate_p)
    log_decay = -8.0 * reset_gate * decay_rate
    decay = jnp.exp(log_decay)
    scaling = jnp.sqrt(-jnp.expm1(2.0 * log_decay))
    update = scaling * input_gate * u_float
    _, states = lax.associative_scan(combine, (decay, update), axis=0)
    output = (x_float + live_mask * states).astype(jnp.bfloat16)
    return (output, (normed, inv_rms, u_float, reset_gate, input_gate, decay, scaling, states, decay_rate))

def layer_backward(upstream, stashed, w_a, w_x, rate_p, gain, live_mask):
    normed, inv_rms, u_float, reset_gate, input_gate, decay, scaling, states, decay_rate = stashed
    d_state = live_mask * upstream
    tail_a, tail_z = lax.associative_scan(combine, (decay, decay * d_state), reverse=True, axis=0)
    z_next = jnp.concatenate([tail_z[1:], jnp.zeros_like(tail_z[:1])], axis=0)
    adjoint = d_state + z_next
    h_prev = jnp.concatenate([jnp.zeros_like(states[:1]), states[:-1]], axis=0)
    d_decay = adjoint * h_prev
    d_input = adjoint * scaling * u_float
    d_log = d_decay * decay - adjoint * input_gate * u_float * decay * decay / scaling
    d_pre_a = d_log * (-8.0 * decay_rate) * reset_gate * (1.0 - reset_gate)
    d_pre_x = d_input * input_gate * (1.0 - input_gate)
    g_rate = lax.optimization_barrier(jnp.sum(d_log * (-8.0 * reset_gate), axis=0)) * jax.nn.sigmoid(rate_p)
    g_bias_a = lax.optimization_barrier(jnp.sum(d_pre_a, axis=0))
    g_bias_x = lax.optimization_barrier(jnp.sum(d_pre_x, axis=0))
    d_normed_in = adjoint * scaling * input_gate
    d_normed_in = d_normed_in + blockdiag_t(d_pre_a.astype(jnp.bfloat16), w_a)
    d_normed_in = d_normed_in + blockdiag_t(d_pre_x.astype(jnp.bfloat16), w_x)
    g_gain = lax.optimization_barrier(jnp.sum(d_normed_in * normed, axis=0))
    d_normed = d_normed_in * gain
    inner = lax.optimization_barrier(jnp.mean(d_normed * normed, axis=-1, keepdims=True))
    downstream = upstream + inv_rms * (d_normed - normed * inner)
    return (downstream, (g_gain, g_bias_a, g_bias_x, g_rate))

def one_section(per_section):
    acts, saved, grads, w_a, w_x, b_a, b_x, rate_p, gain, layer_count = per_section
    current = acts
    for slot_index in range(LSLOT):
        live_mask = (slot_index < layer_count).astype(jnp.float32)
        current, _ = layer_forward(current, w_a[slot_index], w_x[slot_index], b_a[slot_index], b_x[slot_index], rate_p[slot_index], gain[slot_index], live_mask)
    forward_result = current
    recomputed = saved
    stash_list = []
    for slot_index in range(LSLOT):
        live_mask = (slot_index < layer_count).astype(jnp.float32)
        recomputed, stashed = layer_forward(recomputed, w_a[slot_index], w_x[slot_index], b_a[slot_index], b_x[slot_index], rate_p[slot_index], gain[slot_index], live_mask)
        stash_list.append(stashed)
    upstream = grads.astype(jnp.float32)
    grad_lists = [None] * LSLOT
    for slot_index in reversed(range(LSLOT)):
        live_mask = (slot_index < layer_count).astype(jnp.float32)
        upstream, slot_grads = layer_backward(upstream, stash_list[slot_index], w_a[slot_index], w_x[slot_index], rate_p[slot_index], gain[slot_index], live_mask)
        grad_lists[slot_index] = slot_grads
    stacked = tuple((jnp.stack([grad_lists[k][m] for k in range(LSLOT)], axis=0) for m in range(4)))
    return (forward_result, upstream.astype(jnp.bfloat16)) + stacked

def reference(acts_in, saved_in, grad_in, gate_a, gate_x, bias_a, bias_x, rate_param, norm_gain, section_layers):
    results = lax.map(one_section, (acts_in, saved_in, grad_in, gate_a, gate_x, bias_a, bias_x, rate_param, norm_gain, section_layers))
    forward_all, downstream_all, g_gain, g_bias_a, g_bias_x, g_rate = results
    acts_out = jnp.roll(forward_all, 1, axis=0)
    grad_out = jnp.roll(downstream_all, -1, axis=0)
    return (acts_out, grad_out, g_gain, g_bias_a, g_bias_x, g_rate)
```

```python
import jax
import jax.numpy as jnp
from jax import lax
from jax.experimental import pallas as pl
from jax.experimental.pallas import tpu as pltpu
from jax.sharding import Mesh
from jax.sharding import PartitionSpec as P

MESH = pl.DeviceIdType.MESH
F32, BF16 = jnp.float32, jnp.bfloat16
EPS = 1e-06
NX, NY = 4, 8
GROUPS, LANES8 = 16, 8
BLK = 256
STEP = 4
PER_LAYER = 43


def kernel(
    acts_hbm, saved_hbm, grad_hbm, ga_hbm, gx_hbm, bias_a, bias_x, rate_param, gain, layers,
    acts_out, grad_out, o_gain, o_ba, o_bx, o_rate,
    wa, wx, wfull, xin, out_buf,
    x0, x1, inv, ac, hl, st_a, st_r, st_i, st_s, st_rs, qp, bn, dy, dn,
    pre_a, pre_x, ends, par, gsum,
    ey0, ex0, ey1, ex1, ey2, ex2, eyg, exg,
    load_sem, g_send, g_recv, e_send, e_recv, o_send, o_recv,
):
    s, mx, my = lax.axis_index("section"), lax.axis_index("tm_0"), lax.axis_index("tm_1")
    ns = lax.axis_size("section")
    heads = x0.shape[-1] // BLK
    chans = x0.shape[-1]
    pieces = chans // 128

    def xp(d):
        return lax.rem(mx + (d + NX), NX)

    def yp(d):
        return lax.rem(my + (d + NY), NY)

    def at_x(d):
        return (s, xp(d), my)

    def at_y(d):
        return (s, mx, yp(d))

    sec_next = (lax.rem(s + 1, ns), mx, my)
    sec_prev = (lax.rem(s + (ns - 1), ns), mx, my)

    loads = [
        pltpu.make_async_copy(ga_hbm, wa.at[:, mx, my], load_sem.at[0]),
        pltpu.make_async_copy(gx_hbm, wx.at[:, mx, my], load_sem.at[1]),
        pltpu.make_async_copy(saved_hbm, xin.at[0], load_sem.at[2]),
        pltpu.make_async_copy(acts_hbm, xin.at[1], load_sem.at[3]),
        pltpu.make_async_copy(grad_hbm, xin.at[2], load_sem.at[4]),
    ]
    for c in loads:
        c.start()

    barrier = pltpu.get_barrier_semaphore()
    peers = [at_y(d) for d in range(1, NY)] + [at_x(d) for d in range(1, NX)]
    peers += [sec_next, sec_prev]
    for dev in peers:
        pl.semaphore_signal(barrier, inc=1, device_id=dev, device_id_type=MESH)
    pl.semaphore_wait(barrier, len(peers))

    sent = []

    def send(src, dst, sems, k, dev):
        c = pltpu.make_async_remote_copy(
            src_ref=src, dst_ref=dst, send_sem=sems[0].at[k], recv_sem=sems[1].at[k],
            device_id=dev, device_id_type=MESH,
        )
        c.start()
        sent.append(c)

    def arrived(slot, sems, k):
        pltpu.make_async_remote_copy(
            src_ref=slot, dst_ref=slot, send_sem=sems[0].at[k], recv_sem=sems[1].at[k],
            device_id=sec_next, device_id_type=MESH,
        ).wait_recv()

    gsems = (g_send, g_recv)

    def gather(l):
        base = l * PER_LAYER
        kx = lambda d: base + d - 1
        ka = lambda step, side: base + 3 + (step - 1) * 2 + side
        ky = lambda step, side: base + 11 + (step - 1) * 2 + side
        k1 = lambda d, up, side: base + 19 + (0 if d == 0 else (14 if d == 4 else 2 + (d - 1) * 4 + 2 * up)) + side
        k2 = lambda d, up: base + 35 + (0 if d == 0 else (7 if d == 4 else 1 + (d - 1) * 2 + up))

        def go(ref, k, dev):
            send(ref, ref, gsems, k, dev)

        def a_col(y):
            return wa.at[l, :, y]

        def x_piece(x, y):
            return wx.at[l, x, y]

        def x_first(d):
            for up in (0, 1) if d in (1, 2, 3) else (0,):
                y = yp(d if up else -d)
                go(x_piece(mx, y), k1(d, up, 0), at_x(1))
                go(x_piece(mx, y), k1(d, up, 1), at_x(-1))

        def x_first_in(d):
            for up in (0, 1) if d in (1, 2, 3) else (0,):
                y = yp(d if up else -d)
                arrived(x_piece(xp(-1), y), gsems, k1(d, up, 0))
                arrived(x_piece(xp(1), y), gsems, k1(d, up, 1))

        def x_second(d):
            if d != 4:
                go(x_piece(xp(-1), yp(-d)), k2(d, 0), at_x(1))
            if d != 0:
                go(x_piece(xp(1), yp(d)), k2(d, 1 if d != 4 else 0), at_x(-1))

        def x_second_in(d):
            if d != 4:
                arrived(x_piece(xp(2), yp(-d)), gsems, k2(d, 0))
            if d != 0:
                arrived(x_piece(xp(2), yp(d)), gsems, k2(d, 1 if d != 4 else 0))

        half = heads // 2
        lo, hi = slice(0, half), slice(half, heads)
        for d in (1, 3, 2):
            go(wa.at[l, mx, my], kx(d), at_x(d))
        go(x_piece(mx, my), ky(1, 0), at_y(1))
        go(x_piece(mx, my), ky(1, 1), at_y(-1))
        x_first(0)
        yield
        for d in (1, 3, 2):
            arrived(wa.at[l, xp(-d), my], gsems, kx(d))
        go(a_col(my), ka(1, 0), at_y(1))
        go(a_col(my), ka(1, 1), at_y(-1))
        for d in (1, 2, 3):
            if d > 1:
                arrived(a_col(yp(-(d - 1))), gsems, ka(d - 1, 0))
                go(a_col(yp(-(d - 1))), ka(d, 0), at_y(1))
                arrived(a_col(yp(d - 1)), gsems, ka(d - 1, 1))
                go(a_col(yp(d - 1)), ka(d, 1), at_y(-1))
            arrived(x_piece(mx, yp(-d)), gsems, ky(d, 0))
            arrived(x_piece(mx, yp(d)), gsems, ky(d, 1))
            if d < 3:
                go(x_piece(mx, yp(-d)), ky(d + 1, 0), at_y(1))
                go(x_piece(mx, yp(d)), ky(d + 1, 1), at_y(-1))
            else:
                go(wx.at[l, mx, yp(-3), lo], ky(4, 0), at_y(1))
                go(wx.at[l, mx, yp(3), hi], ky(4, 1), at_y(-1))
            x_first(d)
            x_first_in(d - 1)
            x_second(d - 1)
            yield
        arrived(a_col(yp(-3)), gsems, ka(3, 0))
        go(wa.at[l, :, yp(-3), lo], ka(4, 0), at_y(1))
        arrived(a_col(yp(3)), gsems, ka(3, 1))
        go(wa.at[l, :, yp(3), hi], ka(4, 1), at_y(-1))
        arrived(wx.at[l, mx, yp(4), lo], gsems, ky(4, 0))
        arrived(wx.at[l, mx, yp(4), hi], gsems, ky(4, 1))
        x_first(4)
        x_first_in(3)
        x_second(3)
        yield
        x_first_in(4)
        x_second(4)
        for d in (0, 1, 2, 3):
            x_second_in(d)
        yield
        arrived(wa.at[l, :, yp(4), lo], gsems, ka(4, 0))
        arrived(wa.at[l, :, yp(4), hi], gsems, ka(4, 1))
        x_second_in(4)

    esems = (e_send, e_recv)

    class Exchange:
        def __init__(self, number, yb, xb):
            self.base, self.yb, self.xb = number * (NX + NY - 2), yb, xb

        def y_start(self):
            for d in range(1, NY):
                send(self.yb.at[my], self.yb.at[my], esems, self.base + d - 1, at_y(d))

        def y_wait(self):
            for d in range(1, NY):
                arrived(self.yb.at[yp(-d)], esems, self.base + d - 1)

        def x_start(self):
            for d in range(1, NX):
                send(self.xb.at[mx], self.xb.at[mx], esems, self.base + NY - 1 + d - 1, at_x(d))

        def x_wait(self):
            for d in range(1, NX):
                arrived(self.xb.at[xp(-d)], esems, self.base + NY - 1 + d - 1)

    e0 = [Exchange(k, ey0.at[k], ex0.at[k]) for k in (0, 1)]
    e1 = Exchange(2, ey1, ex1)
    e1a = Exchange(3, ey2.at[0], ex2.at[0])
    e2 = Exchange(4, ey2.at[1, :, 0:1], ex2.at[1, :, 0:1])
    eg = [Exchange(5 + l, eyg.at[l], exg.at[l]) for l in (0, 1)]

    y = jnp.exp(rate_param[...])
    rate = y * (1.0 + y * (-1.0 / 2 + y * (1.0 / 3 + y * (-1.0 / 4 + y * (1.0 / 5 + y * (-1.0 / 6))))))
    par[0] = -8.0 * rate
    par[1] = y / (1.0 + y)
    live = [jnp.minimum(jnp.maximum(layers[0] - l, 0), 1).astype(F32) for l in (0, 1)]

    tok = lax.broadcasted_iota(jnp.int32, (128, 128), 1)
    row = lax.broadcasted_iota(jnp.int32, (128, 128), 0)
    to_runs = (tok == (row % LANES8) * GROUPS + row // LANES8).astype(F32).astype(BF16)
    to_tokens = (row == (tok % LANES8) * GROUPS + tok // LANES8).astype(F32).astype(BF16)
    sub = lax.broadcasted_iota(jnp.int32, (LANES8, chans), 0)

    def cols_of(h):
        return pl.ds(pl.multiple_of(h * BLK, BLK), BLK)

    def over_heads(body, lo=0, hi=None):
        def step(h, _):
            body(h, cols_of(h))
            return 0

        lax.fori_loop(lo, heads if hi is None else hi, step, 0)

    def chunks():
        return [pl.ds(c * STEP, STEP) for c in range(GROUPS // STEP)]

    def runs3(v):
        return v.reshape(GROUPS, LANES8, v.shape[-1])

    def rows2(v):
        return v.reshape(GROUPS * LANES8, v.shape[-1])

    def squares(x):
        sq = x * x
        return sq[..., :128] + sq[..., 128:]

    def store_inv(slot, acc):
        mean = jnp.sum(acc, axis=-1, keepdims=True) * (1.0 / chans)
        inv[slot] = jnp.broadcast_to(lax.rsqrt(mean + EPS), inv.shape[1:])

    def permuted(k, dst):
        def step(h, acc):
            cols = cols_of(h)
            x = runs3(jnp.dot(to_runs, xin[k, :, cols], preferred_element_type=F32))
            dst[:, :, cols] = x
            return acc + squares(x)

        return lax.fori_loop(0, heads, step, jnp.zeros((GROUPS, LANES8, 128), F32))

    def sigmoid(v):
        return 1.0 / (1.0 + jnp.exp(-v))

    def forward(l, stream, xref, kk, sl, build, lo, hi):
        def body(h, cols):
            g = gain[pl.ds(l, 1), cols]
            ba, bx = bias_a[pl.ds(l, 1), cols], bias_x[pl.ds(l, 1), cols]
            k8 = par[0, pl.ds(l, 1), cols]
            if build:
                w_a = wa[l, :, :, h].astype(F32).reshape(BLK, BLK).astype(BF16)
                w_x = wx[l, :, :, h].astype(F32).reshape(BLK, BLK).astype(BF16)
                wfull[l, 0, h] = w_a
                wfull[l, 1, h] = w_x
            else:
                w_a, w_x = wfull[l, 0, h], wfull[l, 1, h]
            u = rows2(xref[:, :, cols] * inv[kk] * g).astype(BF16)
            pre_a[...] = runs3(jnp.dot(u, w_a, preferred_element_type=F32))
            pre_x[...] = runs3(jnp.dot(u, w_x, preferred_element_type=F32))
            cum_a = jnp.ones((LANES8, BLK), F32)
            cum_h = jnp.zeros((LANES8, BLK), F32)
            for c, rows in enumerate(chunks()):
                uf = (xref[rows, :, cols] * inv[kk, rows] * g).astype(BF16).astype(F32)
                r = sigmoid(pre_a[rows] + ba)
                i = sigmoid(pre_x[rows] + bx)
                log_a = r * k8
                a = jnp.exp(log_a)
                z = log_a * 2.0
                p = 1.0 / 120 + z * (1.0 / 720)
                p = 1.0 / 24 + z * p
                p = 1.0 / 6 + z * p
                p = 0.5 + z * p
                p = 1.0 + z * p
                w = -(z * p)
                rs = lax.rsqrt(jnp.maximum(w, 1e-36))
                sc = w * rs
                up = sc * i * uf
                if stream == 0:
                    st_a[l, rows, :, cols] = a
                    st_r[l, rows, :, cols] = r
                    st_i[l, rows, :, cols] = i
                    st_s[l, rows, :, cols] = sc
                    st_rs[l, rows, :, cols] = rs
                for t in range(STEP):
                    cum_a = cum_a * a[t]
                    cum_h = a[t] * cum_h + up[t]
                    ac[sl, c * STEP + t + 1, :, cols] = cum_a
                    hl[sl, c * STEP + t + 1, :, cols] = cum_h
            ac[sl, 0, :, cols] = jnp.ones((LANES8, BLK), F32)
            hl[sl, 0, :, cols] = jnp.zeros((LANES8, BLK), F32)

        over_heads(body, lo, hi)

    def shifted(v, n, fill):
        if n > 0:
            return jnp.where(sub >= n, pltpu.roll(v, n, 0), fill)
        return jnp.where(sub < LANES8 + n, pltpu.roll(v, LANES8 + n, 0), fill)

    def joined(a, h, sign):
        for n in (1, 2, 4):
            h = a * shifted(h, sign * n, 0.0) + h
            a = a * shifted(a, sign * n, 1.0)
        return a, h

    def put_summary(dst, k, full, at):
        for g in range(pieces):
            dst[my, k, g : g + 1, :] = full[at : at + 1, 128 * g : 128 * (g + 1)]

    def summarise(sl, dst):
        a, h = joined(ac[sl, GROUPS], hl[sl, GROUPS], 1)
        ends[sl, 0] = shifted(a, 1, 1.0)
        ends[sl, 1] = shifted(h, 1, 0.0)
        put_summary(dst, 0, a, LANES8 - 1)
        put_summary(dst, 1, h, LANES8 - 1)

    def summarise_back(l, dst, k):
        a, z = joined(bn[l, GROUPS], qp[l, GROUPS], -1)
        ends[3 + l, 0] = shifted(a, -1, 1.0)
        ends[3 + l, 1] = shifted(z, -1, 0.0)
        put_summary(dst, k, z, 0)

    def row_total(yb, xb):
        a, h = yb[0, 0], yb[0, 1]
        for t in range(1, NY):
            h = yb[t, 0] * h + yb[t, 1]
            a = yb[t, 0] * a
        xb[mx, 0] = a
        xb[mx, 1] = h

    def row_total_back(ya, yz, kz, xz, kx):
        z = yz[NY - 1, kz]
        for t in reversed(range(NY - 1)):
            z = ya[t, 0] * z + yz[t, kz]
        xz[mx, kx] = z

    def entering(yb, xb):
        h = jnp.zeros((pieces, 128), F32)
        for t in range(NX - 1):
            h = jnp.where(t < mx, xb[t, 0] * h + xb[t, 1], h)
        for t in range(NY - 1):
            h = jnp.where(t < my, yb[t, 0] * h + yb[t, 1], h)
        return h

    def entering_back(ya, xa, yz, xz, kz):
        z = jnp.zeros((pieces, 128), F32)
        for t in reversed(range(1, NX)):
            z = jnp.where(t > mx, xa[t, 0] * z + xz[t, kz], z)
        for t in reversed(range(1, NY)):
            z = jnp.where(t > my, ya[t, 0] * z + yz[t, kz], z)
        return z

    def put_entering(k, h):
        for g in range(pieces):
            c = slice(128 * g, 128 * (g + 1))
            ends[k, 2, :, c] = ends[k, 1, :, c] + ends[k, 0, :, c] * h[g : g + 1]

    def next_layer(src, sl, dst):
        def step(h, acc):
            cols = cols_of(h)
            c = ends[sl, 2, :, cols]
            out = []
            for k in range(GROUPS // STEP):
                rows, later = pl.ds(k * STEP, STEP), pl.ds(k * STEP + 1, STEP)
                st = hl[sl, later, :, cols] + ac[sl, later, :, cols] * c
                x = (src[rows, :, cols] + live[0] * st).astype(BF16).astype(F32)
                dst[rows, :, cols] = x
                out.append(squares(x))
            return acc + jnp.concatenate(out, axis=0)

        return lax.fori_loop(0, heads, step, jnp.zeros((GROUPS, LANES8, 128), F32))

    def last_layer(src, sl):
        def body(h, cols):
            c = ends[sl, 2, :, cols]
            st = hl[sl, pl.ds(1, GROUPS), :, cols] + ac[sl, pl.ds(1, GROUPS), :, cols] * c
            x = rows2(src[:, :, cols] + live[1] * st).astype(BF16)
            out_buf[0, :, cols] = jnp.dot(to_tokens, x, preferred_element_type=F32).astype(BF16)

        over_heads(body)

    def scan_back(l, cols):
        z = jnp.zeros((LANES8, BLK), F32)
        b = jnp.ones((LANES8, BLK), F32)
        for t in reversed(range(GROUPS)):
            q = live[l] * dy[t, :, cols] + z
            qp[l, t, :, cols] = q
            bn[l, t, :, cols] = b
            a = st_a[l, t, :, cols]
            z = a * q
            b = a * b
        qp[l, GROUPS, :, cols] = z
        bn[l, GROUPS, :, cols] = b

    def backward(l, xref):
        def step(h, inner):
            cols = cols_of(h)
            g = gain[pl.ds(l, 1), cols]
            k8 = par[0, pl.ds(l, 1), cols]
            c, zin = ends[l, 2, :, cols], ends[3 + l, 2, :, cols]
            sums = [jnp.zeros((LANES8, BLK), F32) for _ in range(3)]
            for rows in chunks():
                q = qp[l, rows, :, cols] + bn[l, rows, :, cols] * zin
                a, r, i = st_a[l, rows, :, cols], st_r[l, rows, :, cols], st_i[l, rows, :, cols]
                sc, rs = st_s[l, rows, :, cols], st_rs[l, rows, :, cols]
                uf = (xref[rows, :, cols] * inv[l, rows] * g).astype(BF16).astype(F32)
                before = hl[l, rows, :, cols] + ac[l, rows, :, cols] * c
                iu = i * uf
                qs = q * sc
                d_log = q * a * (before - iu * a * rs)
                dr = d_log * r
                d_a = dr * k8 * (1.0 - r)
                d_x = qs * iu * (1.0 - i)
                sums[0] += jnp.sum(d_a, axis=0)
                sums[1] += jnp.sum(d_x, axis=0)
                sums[2] += jnp.sum(dr, axis=0)
                pre_a[rows] = d_a
                pre_x[rows] = d_x
                dn[rows, :, cols] = qs * i
            for k in range(3):
                gsum[l, k, :, cols] = sums[k]
            nt = (((1,), (1,)), ((), ()))
            mixed = lax.dot_general(rows2(pre_a[...]).astype(BF16), wfull[l, 0, h], nt, preferred_element_type=F32)
            mixed += lax.dot_general(rows2(pre_x[...]).astype(BF16), wfull[l, 1, h], nt, preferred_element_type=F32)
            pre_a[...] = runs3(mixed)
            total = jnp.zeros((LANES8, BLK), F32)
            out = []
            for rows in chunks():
                n = xref[rows, :, cols] * inv[l, rows]
                du = dn[rows, :, cols] + pre_a[rows]
                dnn = du * n
                total += jnp.sum(dnn, axis=0)
                dn[rows, :, cols] = du * g
                v = dnn * g
                out.append(v[..., :128] + v[..., 128:])
            gsum[l, 3, :, cols] = total
            return inner + jnp.concatenate(out, axis=0)

        inner = lax.fori_loop(0, heads, step, jnp.zeros((GROUPS, LANES8, 128), F32))
        mean = jnp.sum(inner, axis=-1, keepdims=True) * (1.0 / chans)
        inv[3] = jnp.broadcast_to(mean, inv.shape[1:])

    def through_norm(l, xref, finish):
        def body(h, cols):
            for rows in chunks():
                n = xref[rows, :, cols] * inv[l, rows]
                dy[rows, :, cols] = dy[rows, :, cols] + inv[l, rows] * (dn[rows, :, cols] - n * inv[3, rows])
            finish(cols)

        over_heads(body)

    def send_sums(l):
        scale = -8.0 * par[1, pl.ds(l, 1), :]
        for k, source in enumerate((3, 0, 1, 2)):
            v = jnp.sum(gsum[l, source], axis=0, keepdims=True)
            if k == 3:
                v = v * scale
            put_summary(eyg.at[l], k, v, 0)
        eg[l].y_start()

    def pass_sums(l):
        eg[l].y_wait()
        total = eyg[l, 0]
        for t in range(1, NY):
            total += eyg[l, t]
        exg[l, mx] = total
        eg[l].x_start()

    def put_sums(l):
        eg[l].x_wait()
        total = exg[l, 0]
        for t in range(1, NX):
            total += exg[l, t]
        for k, ref in enumerate((o_gain, o_ba, o_bx, o_rate)):
            for g in range(pieces):
                ref[l : l + 1, 128 * g : 128 * (g + 1)] = total[k, g : g + 1, :]

    half = heads // 2
    loads[0].wait()
    loads[1].wait()
    g0, g1 = gather(0), gather(1)
    step = lambda g: next(g, None)
    step(g0)
    loads[2].wait()
    store_inv(0, permuted(0, x0.at[0]))
    step(g0)
    loads[3].wait()
    store_inv(2, permuted(1, x0.at[1]))
    step(g0)
    loads[4].wait()
    permuted(2, dy)
    step(g0)
    step(g0)
    step(g1)
    step(g0)
    step(g1)
    step(g0)
    step(g0)

    forward(0, 0, x0.at[0], 0, 0, True, 0, half)
    step(g1)
    forward(0, 0, x0.at[0], 0, 0, True, half, heads)
    summarise(0, ey0.at[0])
    e0[0].y_start()
    step(g1)
    forward(0, 1, x0.at[1], 2, 2, False, 0, half)
    step(g1)
    e0[0].y_wait()
    row_total(ey0.at[0], ex0.at[0])
    e0[0].x_start()
    forward(0, 1, x0.at[1], 2, 2, False, half, heads)
    summarise(2, ey0.at[1])
    e0[1].y_start()
    step(g1)
    e0[0].x_wait()
    put_entering(0, entering(ey0.at[0], ex0.at[0]))
    store_inv(1, next_layer(x0.at[0], 0, x1.at[0]))
    step(g1)
    step(g1)
    forward(1, 0, x1.at[0], 1, 1, True, 0, half)
    e0[1].y_wait()
    row_total(ey0.at[1], ex0.at[1])
    e0[1].x_start()
    forward(1, 0, x1.at[0], 1, 1, True, half, heads)
    over_heads(lambda h, cols: scan_back(1, cols))
    summarise(1, ey1)
    summarise_back(1, ey1, 2)
    e1.y_start()
    e0[1].x_wait()
    put_entering(2, entering(ey0.at[1], ex0.at[1]))
    store_inv(2, next_layer(x0.at[1], 2, x1.at[1]))
    e1.y_wait()
    row_total(ey1, ex1)
    row_total_back(ey1, ey1, 2, ex1, 2)
    e1.x_start()
    forward(1, 1, x1.at[1], 2, 2, False, 0, heads)
    summarise(2, ey2.at[0])
    e1a.y_start()
    e1.x_wait()
    put_entering(1, entering(ey1, ex1))
    put_entering(4, entering_back(ey1, ex1, ey1, ex1, 2))
    backward(1, x1.at[0])
    through_norm(1, x1.at[0], lambda cols: scan_back(0, cols))
    summarise_back(0, ey2.at[1], 0)
    e2.y_start()
    e1a.y_wait()
    row_total(ey2.at[0], ex2.at[0])
    e1a.x_start()
    send_sums(1)
    e2.y_wait()
    row_total_back(ey0.at[0], ey2.at[1], 0, ex2.at[1], 0)
    e2.x_start()
    e1a.x_wait()
    put_entering(2, entering(ey2.at[0], ex2.at[0]))
    last_layer(x1.at[1], 2)
    send(out_buf.at[0], acts_out, (o_send, o_recv), 0, sec_next)
    e2.x_wait()
    put_entering(3, entering_back(ey0.at[0], ex0.at[0], ey2.at[1], ex2.at[1], 0))
    backward(0, x0.at[0])
    send_sums(0)
    pass_sums(1)

    def finish(cols):
        out_buf[1, :, cols] = jnp.dot(to_tokens, rows2(dy[:, :, cols]).astype(BF16), preferred_element_type=F32).astype(BF16)

    through_norm(0, x0.at[0], finish)
    send(out_buf.at[1], grad_out, (o_send, o_recv), 1, sec_prev)
    pass_sums(0)
    put_sums(1)
    put_sums(0)
    arrived(acts_out, (o_send, o_recv), 0)
    arrived(grad_out, (o_send, o_recv), 1)
    for c in sent:
        c.wait_send()


def local(acts_in, saved_in, grad_in, gate_a, gate_x, bias_a, bias_x, rate_param, norm_gain, section_layers):
    _, tokens, chans = acts_in.shape
    slots, heads = gate_a.shape[1:3]
    full = (GROUPS, LANES8, chans)
    vec = (chans // 128, 128)
    sem = pltpu.SemaphoreType.DMA
    any_spec = pl.BlockSpec(memory_space=pl.ANY)
    vmem_spec = pl.BlockSpec(memory_space=pltpu.VMEM)
    exchanges = 7 * (NX + NY - 2)
    vm = pltpu.VMEM
    outs = pl.pallas_call(
        kernel,
        out_shape=[jax.ShapeDtypeStruct((tokens, chans), BF16)] * 2
        + [jax.ShapeDtypeStruct((slots, chans), F32)] * 4,
        in_specs=[any_spec] * 5 + [vmem_spec] * 4 + [pl.BlockSpec(memory_space=pltpu.SMEM)],
        out_specs=[any_spec] * 2 + [vmem_spec] * 4,
        scratch_shapes=[
            vm((slots, NX, NY, heads, 8, BLK), BF16),
            vm((slots, NX, NY, heads, 8, BLK), BF16),
            vm((slots, 2, heads, BLK, BLK), BF16),
            vm((3, tokens, chans), BF16),
            vm((2, tokens, chans), BF16),
            vm((2, *full), F32),
            vm((2, *full), F32),
            vm((4, GROUPS, LANES8, BLK), F32),
            vm((3, GROUPS + 1, LANES8, chans), F32),
            vm((3, GROUPS + 1, LANES8, chans), F32),
            vm((slots, *full), F32),
            vm((slots, *full), F32),
            vm((slots, *full), F32),
            vm((slots, *full), F32),
            vm((slots, *full), F32),
            vm((slots, GROUPS + 1, LANES8, chans), F32),
            vm((slots, GROUPS + 1, LANES8, chans), F32),
            vm(full, F32),
            vm(full, F32),
            vm((GROUPS, LANES8, BLK), F32),
            vm((GROUPS, LANES8, BLK), F32),
            vm((5, 3, LANES8, chans), F32),
            vm((2, slots, chans), F32),
            vm((slots, 4, LANES8, chans), F32),
            vm((2, NY, 2, *vec), F32),
            vm((2, NX, 2, *vec), F32),
            vm((NY, 3, *vec), F32),
            vm((NX, 3, *vec), F32),
            vm((2, NY, 2, *vec), F32),
            vm((2, NX, 2, *vec), F32),
            vm((slots, NY, 4, *vec), F32),
            vm((slots, NX, 4, *vec), F32),
            sem((5,)),
            sem((2 * PER_LAYER,)),
            sem((2 * PER_LAYER,)),
            sem((exchanges,)),
            sem((exchanges,)),
            sem((2,)),
            sem((2,)),
        ],
        compiler_params=pltpu.CompilerParams(
            collective_id=0, has_side_effects=True, vmem_limit_bytes=60 * 1024 * 1024
        ),
    )(
        acts_in[0], saved_in[0], grad_in[0], gate_a[0], gate_x[0],
        bias_a[0], bias_x[0], rate_param[0], norm_gain[0], section_layers,
    )
    return tuple(o[None] for o in outs)


def solution(mesh):
    finer = Mesh(mesh.devices.reshape(mesh.shape["section"], NX, NY), ("section", "tm_0", "tm_1"))
    tm = ("tm_0", "tm_1")
    act = P("section", tm, None)
    gate = P("section", None, None, tm, None)
    small = P("section", None, None)
    return jax.shard_map(
        local,
        mesh=finer,
        in_specs=(act, act, act, gate, gate, small, small, small, small, P("section")),
        out_specs=(act, act, small, small, small, small),
        check_vma=False,
    )
```

```python
import jax
import jax.numpy as jnp
from jax import lax
from jax.experimental import pallas as pl
from jax.experimental.pallas import tpu as pltpu
from jax.sharding import Mesh
from jax.sharding import PartitionSpec as P

MESH = pl.DeviceIdType.MESH
F32, BF16 = jnp.float32, jnp.bfloat16
EPS = 1e-06
NX, NY = 4, 8
GROUPS, LANES8 = 16, 8
BLK = 256
STEP = 4


def kernel(
    acts_hbm, saved_hbm, grad_hbm, ga_hbm, gx_hbm, bias_a, bias_x, rate_param, gain, layers,
    acts_out, grad_out, sums_out,
    w, wsrc, wfull, xin, out_buf,
    x0, x1, inv, sq, ac, hl, st_a, st_r, st_i, st_s, st_rs, qp, bn, dy, dn,
    pre_a, pre_x, ends, par, gsum,
    ey0, ey1, ey1a, ey2, eyg, exg, xsum,
    load_sem, w_send, w_recv, i_send, i_recv, e_send, e_recv, n_send, n_recv, g_send, g_recv, o_send, o_recv,
):
    s, mx, my = lax.axis_index("section"), lax.axis_index("tm_0"), lax.axis_index("tm_1")
    ns = lax.axis_size("section")
    chans = x0.shape[-1]
    heads = chans // BLK
    own = chans // NX
    mine = heads // NX
    pieces = chans // 128

    def xp(d):
        return lax.rem(mx + (d + NX), NX)

    def yp(d):
        return lax.rem(my + (d + NY), NY)

    def at_x(d):
        return (s, xp(d), my)

    def at_y(d):
        return (s, mx, yp(d))

    def section(step, d):
        return (lax.rem(s + (step + ns), ns), xp(d), my)

    def part(x):
        return pl.ds(pl.multiple_of(x * own, own), own)

    loads = [
        pltpu.make_async_copy(ga_hbm, wsrc.at[:, :, 0], load_sem.at[0]),
        pltpu.make_async_copy(gx_hbm, wsrc.at[:, :, 1], load_sem.at[1]),
        pltpu.make_async_copy(ga_hbm.at[:, mx], w.at[:, mx, my, 0], load_sem.at[2]),
        pltpu.make_async_copy(gx_hbm.at[:, mx], w.at[:, mx, my, 1], load_sem.at[3]),
    ]
    sources = (saved_hbm, acts_hbm, grad_hbm)
    loads += [
        pltpu.make_async_copy(ref.at[:, part(mx)], xin.at[k, :, part(mx)], load_sem.at[4 + k])
        for k, ref in enumerate(sources)
    ]
    for c in loads:
        c.start()

    around = [(a, b) for b in (0, 1, 7, 2, 6, 3, 5, 4) for a in (0, 1, 3, 2) if a or b]
    peers = [(s, xp(a), yp(b)) for a, b in around]
    peers += [section(step, d) for step in (1, -1) for d in range(NX)]
    barrier = pltpu.get_barrier_semaphore()
    for dev in peers:
        pl.semaphore_signal(barrier, inc=1, device_id=dev, device_id_type=MESH)
    pl.semaphore_wait(barrier, len(peers))

    sent = []

    def send(src, dst, sems, k, dev):
        c = pltpu.make_async_remote_copy(
            src_ref=src, dst_ref=dst, send_sem=sems[0].at[k], recv_sem=sems[1].at[k],
            device_id=dev, device_id_type=MESH,
        )
        c.start()
        sent.append(c)

    def arrived(slot, sems, k):
        pltpu.make_async_remote_copy(
            src_ref=slot, dst_ref=slot, send_sem=sems[0].at[k], recv_sem=sems[1].at[k],
            device_id=at_x(1), device_id_type=MESH,
        ).wait_recv()

    wsems, isems, esems = (w_send, w_recv), (i_send, i_recv), (e_send, e_recv)
    nsems, gsems, osems = (n_send, n_recv), (g_send, g_recv), (o_send, o_recv)

    def inputs_start(k):
        for d in (2, 1, 3):
            send(sources[k].at[:, part(xp(d))], xin.at[k, :, part(mx)], isems, 3 * k + d - 1, at_x(d))

    def inputs_wait(k):
        loads[4 + k].wait()
        for d in (1, 3, 2):
            arrived(xin.at[k, :, part(xp(-d))], isems, 3 * k + d - 1)

    near = [(a, b) for a, b in around if b in (0, 1, 2, NY - 1, NY - 2)]
    per_slot = len(near) + 4

    def weights_start(l):
        for n, (a, b) in enumerate(near):
            send(wsrc.at[l, xp(a)], w.at[l, mx, my], wsems, per_slot * l + n, (s, xp(a), yp(b)))

    def near_wait(l, places):
        for n, (a, b) in enumerate(near):
            if b in places:
                arrived(w.at[l, xp(-a), yp(-b)], wsems, per_slot * l + n)

    lo, hi = slice(0, NX // 2), slice(NX // 2, NX)

    def weights_pass(l):
        near_wait(l, (2, NY - 2))
        k = per_slot * l + len(near)
        for n, (xs, y, d) in enumerate(((lo, -2, 2), (hi, 2, -2), (slice(None), -2, 1), (slice(None), 2, -1))):
            ref = w.at[l, xs, yp(y)]
            send(ref, ref, wsems, k + n, at_y(d))

    def weights_wait(l):
        near_wait(l, (0, 1, NY - 1))
        k = per_slot * l + len(near)
        for n, (xs, y) in enumerate(((lo, 4), (hi, 4), (slice(None), -3), (slice(None), 3))):
            arrived(w.at[l, xs, yp(y)], wsems, k + n)

    class Exchange:
        def __init__(self, number, yb, sems=esems):
            self.base, self.yb, self.sems = number * (NY - 1), yb, sems

        def start(self):
            for d in (4, 3, 5, 2, 6, 1, 7):
                send(self.yb.at[my], self.yb.at[my], self.sems, self.base + d - 1, at_y(d))

        def wait(self):
            for d in range(1, NY):
                arrived(self.yb.at[yp(-d)], self.sems, self.base + d - 1)

    e0 = [Exchange(k, ey0.at[k]) for k in (0, 1)]
    e1 = Exchange(2, ey1)
    e1a = Exchange(3, ey1a)
    e2 = Exchange(4, ey2)
    eg = [Exchange(5 + l, eyg.at[l]) for l in (0, 1)]

    y = jnp.exp(rate_param[...])
    rate = y * (1.0 + y * (-1.0 / 2 + y * (1.0 / 3 + y * (-1.0 / 4 + y * (1.0 / 5 + y * (-1.0 / 6))))))
    par[0] = -8.0 * rate
    par[1] = y / (1.0 + y)
    live = [jnp.minimum(jnp.maximum(layers[0] - l, 0), 1).astype(F32) for l in (0, 1)]

    tok = lax.broadcasted_iota(jnp.int32, (128, 128), 1)
    row = lax.broadcasted_iota(jnp.int32, (128, 128), 0)
    to_runs = (tok == (row % LANES8) * GROUPS + row // LANES8).astype(F32).astype(BF16)
    to_tokens = (row == (tok % LANES8) * GROUPS + tok // LANES8).astype(F32).astype(BF16)
    sub = lax.broadcasted_iota(jnp.int32, (LANES8, chans), 0)
    sub16 = lax.broadcasted_iota(jnp.int32, (pieces, 128), 0)

    def cols_of(h):
        return pl.ds(pl.multiple_of(h * BLK, BLK), BLK)

    def over_heads(body, lo=0, hi=None):
        def step(h, _):
            body(h, cols_of(h))
            return 0

        lax.fori_loop(lo, heads if hi is None else hi, step, 0)

    def chunks():
        return [pl.ds(c * STEP, STEP) for c in range(GROUPS // STEP)]

    def runs3(v):
        return v.reshape(GROUPS, LANES8, v.shape[-1])

    def rows2(v):
        return v.reshape(GROUPS * LANES8, v.shape[-1])

    def squares(x):
        sq = x * x
        return sq[..., :128] + sq[..., 128:]

    def params_of(v):
        return pl.ds(pl.multiple_of((mx * mine + lax.rem(v, mine)) * BLK, BLK), BLK)

    def share(n):
        tile = jnp.zeros((128, 128), F32)
        for b in range(NX):
            both = sq[mine * b]
            for k in range(1, mine):
                both += sq[mine * b + k]
            tile = jnp.where(tok == b, jnp.sum(rows2(both), axis=1, keepdims=True), tile)
        xsum[n, mx] = tile.T[:LANES8]
        for d in (2, 1, 3):
            send(xsum.at[n, mx], xsum.at[n, mx], nsems, 3 * n + d - 1, at_x(d))

    def shared(n):
        for d in (1, 3, 2):
            arrived(xsum.at[n, xp(-d)], nsems, 3 * n + d - 1)
        total = xsum[n, 0]
        for x in range(1, NX):
            total += xsum[n, x]
        return total * (1.0 / chans)

    def put_rows(slot, tile):
        turned = tile.T
        for b in range(NX):
            inv[slot, b] = runs3(jnp.broadcast_to(turned[:, b : b + 1], (128, BLK)))

    def put_inv(slot, n):
        put_rows(slot, lax.rsqrt(shared(n) + EPS))

    def permuted(k, dst, summed):
        def body(v, cols):
            x = runs3(jnp.dot(to_runs, xin[k, :, cols], preferred_element_type=F32))
            dst[:, :, cols] = x
            if summed:
                sq[v] = squares(x)

        over_heads(body)

    def assemble(l):
        for g in (0, 1):
            for k in range(mine):
                wfull[l, g, k] = w[l, :, :, g, k].astype(F32).reshape(BLK, BLK).astype(BF16)

    def sigmoid(v):
        return 1.0 / (1.0 + jnp.exp(-v))

    def forward(l, stream, xref, kk, sl):
        def body(v, cols):
            pc, h, b = params_of(v), lax.rem(v, mine), v // mine
            g = gain[pl.ds(l, 1), pc]
            ba, bx = bias_a[pl.ds(l, 1), pc], bias_x[pl.ds(l, 1), pc]
            k8 = par[0, pl.ds(l, 1), pc]
            w_a, w_x = wfull[l, 0, h], wfull[l, 1, h]
            u = rows2(xref[:, :, cols] * inv[kk, b] * g).astype(BF16)
            pre_a[...] = runs3(jnp.dot(u, w_a, preferred_element_type=F32))
            pre_x[...] = runs3(jnp.dot(u, w_x, preferred_element_type=F32))
            cum_a = jnp.ones((LANES8, BLK), F32)
            cum_h = jnp.zeros((LANES8, BLK), F32)
            for c, rows in enumerate(chunks()):
                uf = (xref[rows, :, cols] * inv[kk, b, rows] * g).astype(BF16).astype(F32)
                r = sigmoid(pre_a[rows] + ba)
                i = sigmoid(pre_x[rows] + bx)
                log_a = r * k8
                a = jnp.exp(log_a)
                z = log_a * 2.0
                p = 1.0 / 120 + z * (1.0 / 720)
                p = 1.0 / 24 + z * p
                p = 1.0 / 6 + z * p
                p = 0.5 + z * p
                p = 1.0 + z * p
                sc2 = -(z * p)
                rs = lax.rsqrt(jnp.maximum(sc2, 1e-36))
                sc = sc2 * rs
                up = sc * i * uf
                if stream == 0:
                    st_a[l, rows, :, cols] = a
                    st_r[l, rows, :, cols] = r
                    st_i[l, rows, :, cols] = i
                    st_s[l, rows, :, cols] = sc
                    st_rs[l, rows, :, cols] = rs
                for t in range(STEP):
                    cum_a = cum_a * a[t]
                    cum_h = a[t] * cum_h + up[t]
                    ac[sl, c * STEP + t + 1, :, cols] = cum_a
                    hl[sl, c * STEP + t + 1, :, cols] = cum_h
            ac[sl, 0, :, cols] = jnp.ones((LANES8, BLK), F32)
            hl[sl, 0, :, cols] = jnp.zeros((LANES8, BLK), F32)

        over_heads(body)

    def shifted(v, n, fill):
        if n > 0:
            return jnp.where(sub >= n, pltpu.roll(v, n, 0), fill)
        return jnp.where(sub < LANES8 + n, pltpu.roll(v, LANES8 + n, 0), fill)

    def joined(a, h, sign):
        for n in (1, 2, 4):
            h = a * shifted(h, sign * n, 0.0) + h
            a = a * shifted(a, sign * n, 1.0)
        return a, h

    def put_summary(dst, k, full, at):
        for g in range(pieces):
            dst[my, k, g : g + 1, :] = full[at : at + 1, 128 * g : 128 * (g + 1)]

    def summarise(sl, dst):
        a, h = joined(ac[sl, GROUPS], hl[sl, GROUPS], 1)
        ends[sl, 0] = shifted(a, 1, 1.0)
        ends[sl, 1] = shifted(h, 1, 0.0)
        put_summary(dst, 0, a, LANES8 - 1)
        put_summary(dst, 1, h, LANES8 - 1)

    def summarise_back(l, dst, k):
        a, z = joined(bn[l, GROUPS], qp[l, GROUPS], -1)
        ends[3 + l, 0] = shifted(a, -1, 1.0)
        ends[3 + l, 1] = shifted(z, -1, 0.0)
        put_summary(dst, k, z, 0)

    def entering(yb):
        a, h = yb[0, 0], yb[0, 1]
        for t in range(1, NY):
            h = yb[t, 0] * h + yb[t, 1]
            a = yb[t, 0] * a
        per = pieces // NX
        state = jnp.zeros((pieces, 128), F32)
        for _ in range(NX - 1):
            state = jnp.where(sub16 >= per, pltpu.roll(a * state + h, per, 0), 0.0)
        for t in range(NY - 1):
            state = jnp.where(t < my, yb[t, 0] * state + yb[t, 1], state)
        return state

    def entering_back(ya, yz, kz):
        z = yz[NY - 1, kz]
        a = ya[NY - 1, 0]
        for t in reversed(range(NY - 1)):
            z = ya[t, 0] * z + yz[t, kz]
            a = ya[t, 0] * a
        per = pieces // NX
        state = jnp.zeros((pieces, 128), F32)
        for _ in range(NX - 1):
            state = jnp.where(sub16 < pieces - per, pltpu.roll(a * state + z, pieces - per, 0), 0.0)
        for t in reversed(range(1, NY)):
            state = jnp.where(t > my, ya[t, 0] * state + yz[t, kz], state)
        return state

    def put_entering(k, h):
        for g in range(pieces):
            c = slice(128 * g, 128 * (g + 1))
            ends[k, 2, :, c] = ends[k, 1, :, c] + ends[k, 0, :, c] * h[g : g + 1]

    def next_layer(src, sl, dst):
        def body(v, cols):
            c = ends[sl, 2, :, cols]
            for k in range(GROUPS // STEP):
                rows, later = pl.ds(k * STEP, STEP), pl.ds(k * STEP + 1, STEP)
                st = hl[sl, later, :, cols] + ac[sl, later, :, cols] * c
                x = (src[rows, :, cols] + live[0] * st).astype(BF16).astype(F32)
                dst[rows, :, cols] = x
                sq[v, rows] = squares(x)

        over_heads(body)

    def last_layer(src, sl):
        def body(h, cols):
            c = ends[sl, 2, :, cols]
            st = hl[sl, pl.ds(1, GROUPS), :, cols] + ac[sl, pl.ds(1, GROUPS), :, cols] * c
            x = rows2(src[:, :, cols] + live[1] * st).astype(BF16)
            out_buf[0, :, cols] = jnp.dot(to_tokens, x, preferred_element_type=F32).astype(BF16)

        over_heads(body)

    def scan_back(l, cols):
        z = jnp.zeros((LANES8, BLK), F32)
        b = jnp.ones((LANES8, BLK), F32)
        for t in reversed(range(GROUPS)):
            q = live[l] * dy[t, :, cols] + z
            qp[l, t, :, cols] = q
            bn[l, t, :, cols] = b
            a = st_a[l, t, :, cols]
            z = a * q
            b = a * b
        qp[l, GROUPS, :, cols] = z
        bn[l, GROUPS, :, cols] = b

    def backward(l, xref):
        def body(v, cols):
            pc, h, b = params_of(v), lax.rem(v, mine), v // mine
            g = gain[pl.ds(l, 1), pc]
            k8 = par[0, pl.ds(l, 1), pc]
            c, zin = ends[l, 2, :, cols], ends[3 + l, 2, :, cols]
            sums = [jnp.zeros((LANES8, BLK), F32) for _ in range(3)]
            for rows in chunks():
                q = qp[l, rows, :, cols] + bn[l, rows, :, cols] * zin
                a, r, i = st_a[l, rows, :, cols], st_r[l, rows, :, cols], st_i[l, rows, :, cols]
                sc, rs = st_s[l, rows, :, cols], st_rs[l, rows, :, cols]
                uf = (xref[rows, :, cols] * inv[l, b, rows] * g).astype(BF16).astype(F32)
                before = hl[l, rows, :, cols] + ac[l, rows, :, cols] * c
                iu = i * uf
                qs = q * sc
                d_log = q * a * (before - iu * a * rs)
                dr = d_log * r
                d_a = dr * k8 * (1.0 - r)
                d_x = qs * iu * (1.0 - i)
                sums[0] += jnp.sum(d_a, axis=0)
                sums[1] += jnp.sum(d_x, axis=0)
                sums[2] += jnp.sum(dr, axis=0)
                pre_a[rows] = d_a
                pre_x[rows] = d_x
                dn[rows, :, cols] = qs * i
            for k in range(3):
                gsum[l, k, :, cols] = sums[k]
            nt = (((1,), (1,)), ((), ()))
            mixed = lax.dot_general(rows2(pre_a[...]).astype(BF16), wfull[l, 0, h], nt, preferred_element_type=F32)
            mixed += lax.dot_general(rows2(pre_x[...]).astype(BF16), wfull[l, 1, h], nt, preferred_element_type=F32)
            pre_a[...] = runs3(mixed)
            total = jnp.zeros((LANES8, BLK), F32)
            for rows in chunks():
                n = xref[rows, :, cols] * inv[l, b, rows]
                du = dn[rows, :, cols] + pre_a[rows]
                dnn = du * n
                total += jnp.sum(dnn, axis=0)
                dn[rows, :, cols] = du * g
                t = dnn * g
                sq[v, rows] = t[..., :128] + t[..., 128:]
            gsum[l, 3, :, cols] = total

        over_heads(body)

    def through_norm(l, xref, finish, lo=0, hi=None):
        def body(v, cols):
            b = v // mine
            for rows in chunks():
                n = xref[rows, :, cols] * inv[l, b, rows]
                dy[rows, :, cols] = dy[rows, :, cols] + inv[l, b, rows] * (dn[rows, :, cols] - n * inv[3, b, rows])
            finish(cols)

        over_heads(body, lo, hi)

    def send_sums(l):
        for k, source in enumerate((3, 0, 1, 2)):
            v = gsum[l, source, :, :own]
            for b in range(1, NX):
                v += gsum[l, source, :, b * own : (b + 1) * own]
            v = jnp.sum(v, axis=0, keepdims=True)
            if k == 3:
                v = v * (-8.0 * par[1, pl.ds(l, 1), part(mx)])
            for g in range(own // 128):
                at = k * (own // 128) + g
                eyg[l, my, at : at + 1, :] = v[:, 128 * g : 128 * (g + 1)]
        eg[l].start()

    def pass_sums(l):
        eg[l].wait()
        total = eyg[l, 0]
        for t in range(1, NY):
            total += eyg[l, t]
        exg[l, mx] = total
        for d in (2, 1, 3):
            send(exg.at[l, mx], exg.at[l, mx], gsems, 3 * l + d - 1, at_x(d))

    def put_sums(l):
        for d in (1, 3, 2):
            arrived(exg.at[l, xp(-d)], gsems, 3 * l + d - 1)
        sums_out[l] = exg[l]

    def deliver(k, result, step, d):
        send(out_buf.at[k, :, part(xp(d))], result.at[:, part(mx)], osems, NX * k + d, section(step, d))

    def delivered(k, result, d):
        arrived(result.at[:, part(xp(-d))], osems, NX * k + d)

    loads[0].wait()
    loads[1].wait()
    inputs_start(0)
    weights_start(0)
    inputs_wait(0)
    permuted(0, x0.at[0], True)
    share(0)
    weights_pass(0)
    weights_start(1)
    inputs_start(1)
    put_inv(0, 0)
    loads[2].wait()
    loads[3].wait()
    weights_wait(0)
    assemble(0)
    forward(0, 0, x0.at[0], 0, 0)
    summarise(0, ey0.at[0])
    e0[0].start()
    inputs_wait(1)
    permuted(1, x0.at[1], True)
    share(1)
    weights_pass(1)
    inputs_start(2)
    put_inv(2, 1)
    forward(0, 1, x0.at[1], 2, 2)
    e0[0].wait()
    put_entering(0, entering(ey0.at[0]))
    next_layer(x0.at[0], 0, x1.at[0])
    share(2)
    summarise(2, ey0.at[1])
    e0[1].start()
    inputs_wait(2)
    permuted(2, dy, False)
    weights_wait(1)
    assemble(1)
    put_inv(1, 2)
    forward(1, 0, x1.at[0], 1, 1)
    over_heads(lambda v, cols: scan_back(1, cols))
    summarise(1, ey1)
    summarise_back(1, ey1, 2)
    e1.start()
    e0[1].wait()
    put_entering(2, entering(ey0.at[1]))
    next_layer(x0.at[1], 2, x1.at[1])
    share(3)
    put_inv(2, 3)
    e1.wait()
    put_entering(1, entering(ey1))
    put_entering(4, entering_back(ey1, ey1, 2))
    backward(1, x1.at[0])
    share(4)
    forward(1, 1, x1.at[1], 2, 2)
    put_rows(3, shared(4))
    through_norm(1, x1.at[0], lambda cols: scan_back(0, cols))
    summarise_back(0, ey2, 0)
    e2.start()
    summarise(2, ey1a)
    e1a.start()
    send_sums(1)
    e2.wait()
    put_entering(3, entering_back(ey0.at[0], ey2, 0))
    backward(0, x0.at[0])
    share(5)
    send_sums(0)
    e1a.wait()
    put_entering(2, entering(ey1a))
    last_layer(x1.at[1], 2)
    for d in (2, 1, 3, 0):
        deliver(0, acts_out, 1, d)
    put_rows(3, shared(5))

    def finish(cols):
        out_buf[1, :, cols] = jnp.dot(to_tokens, rows2(dy[:, :, cols]).astype(BF16), preferred_element_type=F32).astype(BF16)

    for d in (2, 1, 3, 0):
        through_norm(0, x0.at[0], finish, mine * xp(d), mine * xp(d) + mine)
        deliver(1, grad_out, -1, d)
    pass_sums(1)
    pass_sums(0)
    put_sums(1)
    put_sums(0)
    for d in range(NX):
        delivered(0, acts_out, d)
        delivered(1, grad_out, d)
    for c in sent:
        c.wait_send()


def hand_over(acts, grad, sums, acts_out, grad_out, o_gain, o_ba, o_bx, o_rate):
    acts_out[...] = acts[...]
    grad_out[...] = grad[...]
    per = sums.shape[2] // 4
    for k, ref in enumerate((o_gain, o_ba, o_bx, o_rate)):
        for g in range(ref.shape[-1] // 128):
            ref[:, 128 * g : 128 * (g + 1)] = sums[:, g // per, k * per + g % per, :]


def local(acts_in, saved_in, grad_in, gate_a, gate_x, bias_a, bias_x, rate_param, norm_gain, section_layers):
    _, tokens, chans = acts_in.shape
    slots, heads = gate_a.shape[1:3]
    full = (GROUPS, LANES8, chans)
    vec = (chans // 128, 128)
    sem = pltpu.SemaphoreType.DMA
    any_spec = pl.BlockSpec(memory_space=pl.ANY)
    vmem_spec = pl.BlockSpec(memory_space=pltpu.VMEM)
    mine = heads // NX
    vm = pltpu.VMEM
    outs = pl.pallas_call(
        kernel,
        out_shape=[jax.ShapeDtypeStruct((tokens, chans), BF16)] * 2
        + [jax.ShapeDtypeStruct((slots, NX, *vec), F32)],
        in_specs=[any_spec] * 5 + [vmem_spec] * 4 + [pl.BlockSpec(memory_space=pltpu.SMEM)],
        out_specs=[any_spec] * 2 + [vmem_spec],
        scratch_shapes=[
            vm((slots, NX, NY, 2, mine, 8, BLK), BF16),
            vm((slots, NX, 2, mine, 8, BLK), BF16),
            vm((slots, 2, mine, BLK, BLK), BF16),
            vm((3, tokens, chans), BF16),
            vm((2, tokens, chans), BF16),
            vm((2, *full), F32),
            vm((2, *full), F32),
            vm((4, NX, GROUPS, LANES8, BLK), F32),
            vm((heads, GROUPS, LANES8, 128), F32),
            vm((3, GROUPS + 1, LANES8, chans), F32),
            vm((3, GROUPS + 1, LANES8, chans), F32),
            vm((slots, *full), F32),
            vm((slots, *full), F32),
            vm((slots, *full), F32),
            vm((slots, *full), F32),
            vm((slots, *full), F32),
            vm((slots, GROUPS + 1, LANES8, chans), F32),
            vm((slots, GROUPS + 1, LANES8, chans), F32),
            vm(full, F32),
            vm(full, F32),
            vm((GROUPS, LANES8, BLK), F32),
            vm((GROUPS, LANES8, BLK), F32),
            vm((5, 3, LANES8, chans), F32),
            vm((2, slots, chans), F32),
            vm((slots, 4, LANES8, chans), F32),
            vm((2, NY, 2, *vec), F32),
            vm((NY, 3, *vec), F32),
            vm((NY, 2, *vec), F32),
            vm((NY, 1, *vec), F32),
            vm((slots, NY, *vec), F32),
            vm((slots, NX, *vec), F32),
            vm((6, NX, LANES8, 128), F32),
            sem((7,)),
            *[sem((slots * (5 * NX - 1 + 4),))] * 2,
            *[sem((3 * (NX - 1),))] * 2,
            *[sem((7 * (NY - 1),))] * 2,
            *[sem((6 * (NX - 1),))] * 2,
            *[sem((slots * (NX - 1),))] * 2,
            *[sem((2 * NX,))] * 2,
        ],
        compiler_params=pltpu.CompilerParams(
            collective_id=0, has_side_effects=True, vmem_limit_bytes=60 * 1024 * 1024
        ),
    )(
        acts_in[0], saved_in[0], grad_in[0],
        *(g[0].reshape(slots, NX, mine, 8, BLK) for g in (gate_a, gate_x)),
        bias_a[0], bias_x[0], rate_param[0], norm_gain[0], section_layers,
    )
    outs = pl.pallas_call(
        hand_over,
        out_shape=[jax.ShapeDtypeStruct((tokens, chans), BF16)] * 2
        + [jax.ShapeDtypeStruct((slots, chans), F32)] * 4,
        in_specs=[vmem_spec] * 3,
        out_specs=[vmem_spec] * 6,
    )(*outs)
    return tuple(o[None] for o in outs)


def solution(mesh):
    finer = Mesh(mesh.devices.reshape(mesh.shape["section"], NX, NY), ("section", "tm_0", "tm_1"))
    tm = ("tm_0", "tm_1")
    act = P("section", tm, None)
    gate = P("section", None, None, tm, None)
    small = P("section", None, None)
    return jax.shard_map(
        local,
        mesh=finer,
        in_specs=(act, act, act, gate, gate, small, small, small, small, P("section")),
        out_specs=(act, act, small, small, small, small),
        check_vma=False,
    )
```

```python
import jax
import jax.numpy as jnp
from jax import lax
from jax.experimental import pallas as pl
from jax.experimental.pallas import tpu as pltpu
from jax.sharding import Mesh
from jax.sharding import PartitionSpec as P

MESH = pl.DeviceIdType.MESH
F32, BF16 = jnp.float32, jnp.bfloat16
EPS = 1e-06
NX, NY = 4, 8
GROUPS, LANES8 = 16, 8
BLK = 256
STEP = 4


def kernel(
    acts_hbm, saved_hbm, grad_hbm, ga_hbm, gx_hbm, bias_a, bias_x, rate_param, gain, layers,
    acts_out, grad_out, sums_out,
    w, wsrc, wfull, xin, out_buf,
    x0, x1, inv, sq, ac, hl, st_a, st_r, st_i, st_s, st_rs, qp, bn, dy, dn,
    pre_a, pre_x, ends, par, gsum,
    lines, ey0, ey1, ey1a, ey2, eyg, exg, xsum,
    load_sem, w_send, w_recv, i_send, i_recv, e_send, e_recv, n_send, n_recv, g_send, g_recv, o_send, o_recv,
):
    s, mx, my = lax.axis_index("section"), lax.axis_index("tm_0"), lax.axis_index("tm_1")
    ns = lax.axis_size("section")
    chans = x0.shape[-1]
    heads = chans // BLK
    own = chans // NX
    mine = heads // NX
    pieces = chans // 128

    def xp(d):
        return lax.rem(mx + (d + NX), NX)

    def yp(d):
        return lax.rem(my + (d + NY), NY)

    def at_x(d):
        return (s, xp(d), my)

    def at_y(d):
        return (s, mx, yp(d))

    def section(step, d):
        return (lax.rem(s + (step + ns), ns), xp(d), my)

    def part(x):
        return pl.ds(pl.multiple_of(x * own, own), own)

    loads = [
        pltpu.make_async_copy(ga_hbm, wsrc.at[:, :, 0], load_sem.at[0]),
        pltpu.make_async_copy(gx_hbm, wsrc.at[:, :, 1], load_sem.at[1]),
        pltpu.make_async_copy(ga_hbm.at[:, mx], w.at[:, mx, my, 0], load_sem.at[2]),
        pltpu.make_async_copy(gx_hbm.at[:, mx], w.at[:, mx, my, 1], load_sem.at[3]),
    ]
    sources = (saved_hbm, acts_hbm, grad_hbm)
    loads += [
        pltpu.make_async_copy(ref.at[:, part(mx)], xin.at[k, :, part(mx)], load_sem.at[4 + k])
        for k, ref in enumerate(sources)
    ]
    for c in loads:
        c.start()

    around = [(a, b) for b in (0, 1, 7, 2, 6, 3, 5, 4) for a in (0, 1, 3, 2) if a or b]
    peers = [(s, xp(a), yp(b)) for a, b in around]
    peers += [section(step, d) for step in (1, -1) for d in range(NX)]
    barrier = pltpu.get_barrier_semaphore()
    for dev in peers:
        pl.semaphore_signal(barrier, inc=1, device_id=dev, device_id_type=MESH)
    pl.semaphore_wait(barrier, len(peers))

    sent = []

    def send(src, dst, sems, k, dev):
        c = pltpu.make_async_remote_copy(
            src_ref=src, dst_ref=dst, send_sem=sems[0].at[k], recv_sem=sems[1].at[k],
            device_id=dev, device_id_type=MESH,
        )
        c.start()
        sent.append(c)

    def arrived(slot, sems, k):
        pltpu.make_async_remote_copy(
            src_ref=slot, dst_ref=slot, send_sem=sems[0].at[k], recv_sem=sems[1].at[k],
            device_id=at_x(1), device_id_type=MESH,
        ).wait_recv()

    wsems, isems, esems = (w_send, w_recv), (i_send, i_recv), (e_send, e_recv)
    nsems, gsems, osems = (n_send, n_recv), (g_send, g_recv), (o_send, o_recv)

    def inputs_start(k):
        for d in (2, 1, 3):
            send(sources[k].at[:, part(xp(d))], xin.at[k, :, part(mx)], isems, 3 * k + d - 1, at_x(d))

    def inputs_wait(k):
        loads[4 + k].wait()
        for d in (1, 3, 2):
            arrived(xin.at[k, :, part(xp(-d))], isems, 3 * k + d - 1)

    near = [(a, b) for a, b in around if b in (0, 1, 2, NY - 1, NY - 2)]
    per_slot = len(near) + 4

    def weights_start(l):
        for n, (a, b) in enumerate(near):
            send(wsrc.at[l, xp(a)], w.at[l, mx, my], wsems, per_slot * l + n, (s, xp(a), yp(b)))

    def near_wait(l, places):
        for n, (a, b) in enumerate(near):
            if b in places:
                arrived(w.at[l, xp(-a), yp(-b)], wsems, per_slot * l + n)

    lo, hi = slice(0, NX // 2), slice(NX // 2, NX)

    def weights_pass(l):
        near_wait(l, (2, NY - 2))
        k = per_slot * l + len(near)
        for n, (xs, y, d) in enumerate(((lo, -2, 2), (hi, 2, -2), (slice(None), -2, 1), (slice(None), 2, -1))):
            ref = w.at[l, xs, yp(y)]
            send(ref, ref, wsems, k + n, at_y(d))

    def weights_wait(l):
        near_wait(l, (0, 1, NY - 1))
        k = per_slot * l + len(near)
        for n, (xs, y) in enumerate(((lo, 4), (hi, 4), (slice(None), -3), (slice(None), 3))):
            arrived(w.at[l, xs, yp(y)], wsems, k + n)

    class Exchange:
        def __init__(self, number, yb, sems=esems):
            self.base, self.yb, self.sems = number * (NY - 1), yb, sems

        def start(self):
            for d in (4, 3, 5, 2, 6, 1, 7):
                send(self.yb.at[my], self.yb.at[my], self.sems, self.base + d - 1, at_y(d))

        def wait(self):
            for d in range(1, NY):
                arrived(self.yb.at[yp(-d)], self.sems, self.base + d - 1)

    e0 = [Exchange(k, ey0.at[k]) for k in (0, 1)]
    e1 = Exchange(2, ey1)
    e1a = Exchange(3, ey1a)
    e2 = Exchange(4, ey2)
    eg = [Exchange(5 + l, eyg.at[l]) for l in (0, 1)]

    y = jnp.exp(rate_param[...])
    rate = y * (1.0 + y * (-1.0 / 2 + y * (1.0 / 3 + y * (-1.0 / 4 + y * (1.0 / 5 + y * (-1.0 / 6))))))
    par[0] = -8.0 * rate
    par[1] = y / (1.0 + y)
    live = [jnp.minimum(jnp.maximum(layers[0] - l, 0), 1).astype(F32) for l in (0, 1)]

    tok = lax.broadcasted_iota(jnp.int32, (128, 128), 1)
    row = lax.broadcasted_iota(jnp.int32, (128, 128), 0)
    to_runs = (tok == (row % LANES8) * GROUPS + row // LANES8).astype(F32).astype(BF16)
    to_tokens = (row == (tok % LANES8) * GROUPS + tok // LANES8).astype(F32).astype(BF16)
    sub = lax.broadcasted_iota(jnp.int32, (LANES8, chans), 0)
    sub16 = lax.broadcasted_iota(jnp.int32, (pieces, 128), 0)

    def cols_of(h):
        return pl.ds(pl.multiple_of(h * BLK, BLK), BLK)

    def over_heads(body, lo=0, hi=None):
        def step(h, _):
            body(h, cols_of(h))
            return 0

        lax.fori_loop(lo, heads if hi is None else hi, step, 0)

    def chunks():
        return [pl.ds(c * STEP, STEP) for c in range(GROUPS // STEP)]

    def runs3(v):
        return v.reshape(GROUPS, LANES8, v.shape[-1])

    def rows2(v):
        return v.reshape(GROUPS * LANES8, v.shape[-1])

    def squares(x):
        sq = x * x
        return sq[..., :128] + sq[..., 128:]

    def params_of(h):
        return pl.ds(pl.multiple_of((mx * mine + h) * BLK, BLK), BLK)

    def over_blocks(body):
        def step(b, _):
            for h in range(mine):
                body(b * mine + h, cols_of(b * mine + h), h, b)
            return 0

        lax.fori_loop(0, NX, step, 0)

    def share(n):
        tile = jnp.zeros((128, 128), F32)
        for b in range(NX):
            both = sq[mine * b]
            for k in range(1, mine):
                both += sq[mine * b + k]
            tile = jnp.where(tok == b, jnp.sum(rows2(both), axis=1, keepdims=True), tile)
        xsum[n, mx] = tile.T[:LANES8]
        for d in (2, 1, 3):
            send(xsum.at[n, mx], xsum.at[n, mx], nsems, 3 * n + d - 1, at_x(d))

    def shared(n):
        for d in (1, 3, 2):
            arrived(xsum.at[n, xp(-d)], nsems, 3 * n + d - 1)
        total = xsum[n, 0]
        for x in range(1, NX):
            total += xsum[n, x]
        return total * (1.0 / chans)

    def put_rows(slot, tile):
        turned = tile.T
        for b in range(NX):
            inv[slot, b] = runs3(jnp.broadcast_to(turned[:, b : b + 1], (128, BLK)))

    def put_inv(slot, n):
        put_rows(slot, lax.rsqrt(shared(n) + EPS))

    def permuted(k, dst, summed):
        def body(v, cols):
            x = runs3(jnp.dot(to_runs, xin[k, :, cols], preferred_element_type=F32))
            dst[:, :, cols] = x
            if summed:
                sq[v] = squares(x)

        over_heads(body)

    def assemble(l):
        for g in (0, 1):
            for k in range(mine):
                wfull[l, g, k] = w[l, :, :, g, k].astype(F32).reshape(BLK, BLK).astype(BF16)

    def sigmoid(v):
        return 1.0 / (1.0 + jnp.exp(-v))

    def forward(l, stream, xref, kk, sl):
        def body(v, cols, h, b):
            pc = params_of(h)
            g = gain[pl.ds(l, 1), pc]
            ba, bx = bias_a[pl.ds(l, 1), pc], bias_x[pl.ds(l, 1), pc]
            k8 = par[0, pl.ds(l, 1), pc]
            w_a, w_x = wfull[l, 0, h], wfull[l, 1, h]
            u = rows2(xref[:, :, cols] * inv[kk, b] * g).astype(BF16)
            pre_a[h] = runs3(jnp.dot(u, w_a, preferred_element_type=F32))
            pre_x[h] = runs3(jnp.dot(u, w_x, preferred_element_type=F32))
            cum_a = jnp.ones((LANES8, BLK), F32)
            cum_h = jnp.zeros((LANES8, BLK), F32)
            for c, rows in enumerate(chunks()):
                uf = (xref[rows, :, cols] * inv[kk, b, rows] * g).astype(BF16).astype(F32)
                r = sigmoid(pre_a[h, rows] + ba)
                i = sigmoid(pre_x[h, rows] + bx)
                log_a = r * k8
                a = jnp.exp(log_a)
                z = log_a * 2.0
                p = 1.0 / 120 + z * (1.0 / 720)
                p = 1.0 / 24 + z * p
                p = 1.0 / 6 + z * p
                p = 0.5 + z * p
                p = 1.0 + z * p
                sc2 = -(z * p)
                rs = lax.rsqrt(jnp.maximum(sc2, 1e-36))
                sc = sc2 * rs
                up = sc * i * uf
                if stream == 0:
                    st_a[l, rows, :, cols] = a
                    st_r[l, rows, :, cols] = r
                    st_i[l, rows, :, cols] = i
                    st_s[l, rows, :, cols] = sc
                    st_rs[l, rows, :, cols] = rs
                for t in range(STEP):
                    cum_a = cum_a * a[t]
                    cum_h = a[t] * cum_h + up[t]
                    ac[sl, c * STEP + t + 1, :, cols] = cum_a
                    hl[sl, c * STEP + t + 1, :, cols] = cum_h
            ac[sl, 0, :, cols] = jnp.ones((LANES8, BLK), F32)
            hl[sl, 0, :, cols] = jnp.zeros((LANES8, BLK), F32)

        over_blocks(body)

    def shifted(v, n, fill):
        if n > 0:
            return jnp.where(sub >= n, pltpu.roll(v, n, 0), fill)
        return jnp.where(sub < LANES8 + n, pltpu.roll(v, LANES8 + n, 0), fill)

    def joined(a, h, sign):
        for n in (1, 2, 4):
            h = a * shifted(h, sign * n, 0.0) + h
            a = a * shifted(a, sign * n, 1.0)
        return a, h

    def put_summary(dst, k, full, at):
        for g in range(pieces):
            lines[k, g : g + 1, :] = full[at : at + 1, 128 * g : 128 * (g + 1)]
        dst[my, k] = lines[k].astype(BF16)

    def summarise(sl, dst):
        a, h = joined(ac[sl, GROUPS], hl[sl, GROUPS], 1)
        ends[sl, 0] = shifted(a, 1, 1.0)
        ends[sl, 1] = shifted(h, 1, 0.0)
        put_summary(dst, 0, jnp.log(a), LANES8 - 1)
        put_summary(dst, 1, h, LANES8 - 1)

    def summarise_back(l, dst, k):
        a, z = joined(bn[l, GROUPS], qp[l, GROUPS], -1)
        ends[3 + l, 0] = shifted(a, -1, 1.0)
        ends[3 + l, 1] = shifted(z, -1, 0.0)
        put_summary(dst, k, z, 0)

    def read(y, k):
        vals = [y[t, k].astype(F32) for t in range(NY)]
        return [jnp.exp(v) for v in vals] if k == 0 else vals

    def entering(yb):
        ya, yh = read(yb, 0), read(yb, 1)
        a, h = ya[0], yh[0]
        for t in range(1, NY):
            h = ya[t] * h + yh[t]
            a = ya[t] * a
        per = pieces // NX
        state = jnp.zeros((pieces, 128), F32)
        for _ in range(NX - 1):
            state = jnp.where(sub16 >= per, pltpu.roll(a * state + h, per, 0), 0.0)
        for t in range(NY - 1):
            state = jnp.where(t < my, ya[t] * state + yh[t], state)
        return state

    def entering_back(first, second, kz):
        ya = read(first, 0)
        yz = [second[t, kz].astype(F32) for t in range(NY)]
        a, z = ya[NY - 1], yz[NY - 1]
        for t in reversed(range(NY - 1)):
            z = ya[t] * z + yz[t]
            a = ya[t] * a
        per = pieces // NX
        state = jnp.zeros((pieces, 128), F32)
        for _ in range(NX - 1):
            state = jnp.where(sub16 < pieces - per, pltpu.roll(a * state + z, pieces - per, 0), 0.0)
        for t in reversed(range(1, NY)):
            state = jnp.where(t > my, ya[t] * state + yz[t], state)
        return state

    def put_entering(k, h):
        for g in range(pieces):
            c = slice(128 * g, 128 * (g + 1))
            ends[k, 2, :, c] = ends[k, 1, :, c] + ends[k, 0, :, c] * h[g : g + 1]

    def next_layer(src, sl, dst):
        def body(v, cols):
            c = ends[sl, 2, :, cols]
            for k in range(GROUPS // STEP):
                rows, later = pl.ds(k * STEP, STEP), pl.ds(k * STEP + 1, STEP)
                st = hl[sl, later, :, cols] + ac[sl, later, :, cols] * c
                x = (src[rows, :, cols] + live[0] * st).astype(BF16).astype(F32)
                dst[rows, :, cols] = x
                sq[v, rows] = squares(x)

        over_heads(body)

    def last_layer(src, sl):
        def body(h, cols):
            c = ends[sl, 2, :, cols]
            st = hl[sl, pl.ds(1, GROUPS), :, cols] + ac[sl, pl.ds(1, GROUPS), :, cols] * c
            x = rows2(src[:, :, cols] + live[1] * st).astype(BF16)
            out_buf[0, :, cols] = jnp.dot(to_tokens, x, preferred_element_type=F32).astype(BF16)

        over_heads(body)

    def scan_back(l, cols):
        z = jnp.zeros((LANES8, BLK), F32)
        b = jnp.ones((LANES8, BLK), F32)
        for t in reversed(range(GROUPS)):
            q = live[l] * dy[t, :, cols] + z
            qp[l, t, :, cols] = q
            bn[l, t, :, cols] = b
            a = st_a[l, t, :, cols]
            z = a * q
            b = a * b
        qp[l, GROUPS, :, cols] = z
        bn[l, GROUPS, :, cols] = b

    def backward(l, xref):
        def body(v, cols, h, b):
            pc = params_of(h)
            g = gain[pl.ds(l, 1), pc]
            k8 = par[0, pl.ds(l, 1), pc]
            c, zin = ends[l, 2, :, cols], ends[3 + l, 2, :, cols]
            sums = [jnp.zeros((LANES8, BLK), F32) for _ in range(3)]
            for rows in chunks():
                q = qp[l, rows, :, cols] + bn[l, rows, :, cols] * zin
                a, r, i = st_a[l, rows, :, cols], st_r[l, rows, :, cols], st_i[l, rows, :, cols]
                sc, rs = st_s[l, rows, :, cols], st_rs[l, rows, :, cols]
                uf = (xref[rows, :, cols] * inv[l, b, rows] * g).astype(BF16).astype(F32)
                before = hl[l, rows, :, cols] + ac[l, rows, :, cols] * c
                iu = i * uf
                qs = q * sc
                d_log = q * a * (before - iu * a * rs)
                dr = d_log * r
                d_a = dr * k8 * (1.0 - r)
                d_x = qs * iu * (1.0 - i)
                sums[0] += jnp.sum(d_a, axis=0)
                sums[1] += jnp.sum(d_x, axis=0)
                sums[2] += jnp.sum(dr, axis=0)
                pre_a[h, rows] = d_a
                pre_x[h, rows] = d_x
                dn[rows, :, cols] = qs * i
            for k in range(3):
                gsum[l, k, :, cols] = sums[k]
            nt = (((1,), (1,)), ((), ()))
            mixed = lax.dot_general(rows2(pre_a[h]).astype(BF16), wfull[l, 0, h], nt, preferred_element_type=F32)
            mixed += lax.dot_general(rows2(pre_x[h]).astype(BF16), wfull[l, 1, h], nt, preferred_element_type=F32)
            pre_a[h] = runs3(mixed)
            total = jnp.zeros((LANES8, BLK), F32)
            for rows in chunks():
                n = xref[rows, :, cols] * inv[l, b, rows]
                du = dn[rows, :, cols] + pre_a[h, rows]
                dnn = du * n
                total += jnp.sum(dnn, axis=0)
                dn[rows, :, cols] = du * g
                t = dnn * g
                sq[v, rows] = t[..., :128] + t[..., 128:]
            gsum[l, 3, :, cols] = total

        over_blocks(body)

    def through_norm(l, xref, finish, lo=0, hi=None):
        def body(v, cols):
            b = v // mine
            for rows in chunks():
                n = xref[rows, :, cols] * inv[l, b, rows]
                dy[rows, :, cols] = dy[rows, :, cols] + inv[l, b, rows] * (dn[rows, :, cols] - n * inv[3, b, rows])
            finish(cols)

        over_heads(body, lo, hi)

    def send_sums(l):
        for k, source in enumerate((3, 0, 1, 2)):
            v = gsum[l, source, :, :own]
            for b in range(1, NX):
                v += gsum[l, source, :, b * own : (b + 1) * own]
            v = jnp.sum(v, axis=0, keepdims=True)
            if k == 3:
                v = v * (-8.0 * par[1, pl.ds(l, 1), part(mx)])
            for g in range(own // 128):
                at = k * (own // 128) + g
                eyg[l, my, at : at + 1, :] = v[:, 128 * g : 128 * (g + 1)]
        eg[l].start()

    def pass_sums(l):
        eg[l].wait()
        total = eyg[l, 0]
        for t in range(1, NY):
            total += eyg[l, t]
        exg[l, mx] = total
        for d in (2, 1, 3):
            send(exg.at[l, mx], exg.at[l, mx], gsems, 3 * l + d - 1, at_x(d))

    def put_sums(l):
        for d in (1, 3, 2):
            arrived(exg.at[l, xp(-d)], gsems, 3 * l + d - 1)
        sums_out[l] = exg[l]

    def deliver(k, result, step, d):
        send(out_buf.at[k, :, part(xp(d))], result.at[:, part(mx)], osems, NX * k + d, section(step, d))

    def delivered(k, result, d):
        arrived(result.at[:, part(xp(-d))], osems, NX * k + d)

    loads[0].wait()
    loads[1].wait()
    inputs_start(0)
    weights_start(0)
    inputs_wait(0)
    permuted(0, x0.at[0], True)
    share(0)
    weights_pass(0)
    weights_start(1)
    inputs_start(1)
    put_inv(0, 0)
    loads[2].wait()
    loads[3].wait()
    weights_wait(0)
    assemble(0)
    forward(0, 0, x0.at[0], 0, 0)
    summarise(0, ey0.at[0])
    e0[0].start()
    inputs_wait(1)
    permuted(1, x0.at[1], True)
    share(1)
    weights_pass(1)
    inputs_start(2)
    put_inv(2, 1)
    forward(0, 1, x0.at[1], 2, 2)
    e0[0].wait()
    put_entering(0, entering(ey0.at[0]))
    next_layer(x0.at[0], 0, x1.at[0])
    share(2)
    summarise(2, ey0.at[1])
    e0[1].start()
    inputs_wait(2)
    permuted(2, dy, False)
    weights_wait(1)
    assemble(1)
    put_inv(1, 2)
    forward(1, 0, x1.at[0], 1, 1)
    over_heads(lambda v, cols: scan_back(1, cols))
    summarise(1, ey1)
    summarise_back(1, ey1, 2)
    e1.start()
    e0[1].wait()
    put_entering(2, entering(ey0.at[1]))
    next_layer(x0.at[1], 2, x1.at[1])
    share(3)
    put_inv(2, 3)
    e1.wait()
    put_entering(1, entering(ey1))
    put_entering(4, entering_back(ey1, ey1, 2))
    backward(1, x1.at[0])
    share(4)
    forward(1, 1, x1.at[1], 2, 2)
    put_rows(3, shared(4))
    through_norm(1, x1.at[0], lambda cols: scan_back(0, cols))
    summarise_back(0, ey2, 0)
    e2.start()
    summarise(2, ey1a)
    e1a.start()
    send_sums(1)
    e2.wait()
    put_entering(3, entering_back(ey0.at[0], ey2, 0))
    backward(0, x0.at[0])
    share(5)
    send_sums(0)
    e1a.wait()
    put_entering(2, entering(ey1a))
    last_layer(x1.at[1], 2)
    for d in (2, 1, 3, 0):
        deliver(0, acts_out, 1, d)
    put_rows(3, shared(5))

    def finish(cols):
        out_buf[1, :, cols] = jnp.dot(to_tokens, rows2(dy[:, :, cols]).astype(BF16), preferred_element_type=F32).astype(BF16)

    for d in (2, 1, 3, 0):
        through_norm(0, x0.at[0], finish, mine * xp(d), mine * xp(d) + mine)
        deliver(1, grad_out, -1, d)
    pass_sums(1)
    pass_sums(0)
    put_sums(1)
    put_sums(0)
    for d in range(NX):
        delivered(0, acts_out, d)
        delivered(1, grad_out, d)
    for c in sent:
        c.wait_send()


def hand_over(acts, grad, sums, acts_out, grad_out, o_gain, o_ba, o_bx, o_rate):
    acts_out[...] = acts[...]
    grad_out[...] = grad[...]
    per = sums.shape[2] // 4
    for k, ref in enumerate((o_gain, o_ba, o_bx, o_rate)):
        for g in range(ref.shape[-1] // 128):
            ref[:, 128 * g : 128 * (g + 1)] = sums[:, g // per, k * per + g % per, :]


def local(acts_in, saved_in, grad_in, gate_a, gate_x, bias_a, bias_x, rate_param, norm_gain, section_layers):
    _, tokens, chans = acts_in.shape
    slots, heads = gate_a.shape[1:3]
    full = (GROUPS, LANES8, chans)
    vec = (chans // 128, 128)
    sem = pltpu.SemaphoreType.DMA
    any_spec = pl.BlockSpec(memory_space=pl.ANY)
    vmem_spec = pl.BlockSpec(memory_space=pltpu.VMEM)
    mine = heads // NX
    vm = pltpu.VMEM
    outs = pl.pallas_call(
        kernel,
        out_shape=[jax.ShapeDtypeStruct((tokens, chans), BF16)] * 2
        + [jax.ShapeDtypeStruct((slots, NX, *vec), F32)],
        in_specs=[any_spec] * 5 + [vmem_spec] * 4 + [pl.BlockSpec(memory_space=pltpu.SMEM)],
        out_specs=[any_spec] * 2 + [vmem_spec],
        scratch_shapes=[
            vm((slots, NX, NY, 2, mine, 8, BLK), BF16),
            vm((slots, NX, 2, mine, 8, BLK), BF16),
            vm((slots, 2, mine, BLK, BLK), BF16),
            vm((3, tokens, chans), BF16),
            vm((2, tokens, chans), BF16),
            vm((2, *full), F32),
            vm((2, *full), F32),
            vm((4, NX, GROUPS, LANES8, BLK), F32),
            vm((heads, GROUPS, LANES8, 128), F32),
            vm((3, GROUPS + 1, LANES8, chans), F32),
            vm((3, GROUPS + 1, LANES8, chans), F32),
            vm((slots, *full), F32),
            vm((slots, *full), F32),
            vm((slots, *full), F32),
            vm((slots, *full), F32),
            vm((slots, *full), F32),
            vm((slots, GROUPS + 1, LANES8, chans), F32),
            vm((slots, GROUPS + 1, LANES8, chans), F32),
            vm(full, F32),
            vm(full, F32),
            vm((mine, GROUPS, LANES8, BLK), F32),
            vm((mine, GROUPS, LANES8, BLK), F32),
            vm((5, 3, LANES8, chans), F32),
            vm((2, slots, chans), F32),
            vm((slots, 4, LANES8, chans), F32),
            vm((3, *vec), F32),
            vm((2, NY, 2, *vec), BF16),
            vm((NY, 3, *vec), BF16),
            vm((NY, 2, *vec), BF16),
            vm((NY, 1, *vec), BF16),
            vm((slots, NY, *vec), F32),
            vm((slots, NX, *vec), F32),
            vm((6, NX, LANES8, 128), F32),
            sem((7,)),
            *[sem((slots * (5 * NX - 1 + 4),))] * 2,
            *[sem((3 * (NX - 1),))] * 2,
            *[sem((7 * (NY - 1),))] * 2,
            *[sem((6 * (NX - 1),))] * 2,
            *[sem((slots * (NX - 1),))] * 2,
            *[sem((2 * NX,))] * 2,
        ],
        compiler_params=pltpu.CompilerParams(
            collective_id=0, has_side_effects=True, vmem_limit_bytes=60 * 1024 * 1024
        ),
    )(
        acts_in[0], saved_in[0], grad_in[0],
        *(g[0].reshape(slots, NX, mine, 8, BLK) for g in (gate_a, gate_x)),
        bias_a[0], bias_x[0], rate_param[0], norm_gain[0], section_layers,
    )
    outs = pl.pallas_call(
        hand_over,
        out_shape=[jax.ShapeDtypeStruct((tokens, chans), BF16)] * 2
        + [jax.ShapeDtypeStruct((slots, chans), F32)] * 4,
        in_specs=[vmem_spec] * 3,
        out_specs=[vmem_spec] * 6,
    )(*outs)
    return tuple(o[None] for o in outs)


def solution(mesh):
    finer = Mesh(mesh.devices.reshape(mesh.shape["section"], NX, NY), ("section", "tm_0", "tm_1"))
    tm = ("tm_0", "tm_1")
    act = P("section", tm, None)
    gate = P("section", None, None, tm, None)
    small = P("section", None, None)
    return jax.shard_map(
        local,
        mesh=finer,
        in_specs=(act, act, act, gate, gate, small, small, small, small, P("section")),
        out_specs=(act, act, small, small, small, small),
        check_vma=False,
    )
```

```python
import jax
import jax.numpy as jnp
from jax import lax
from jax.experimental import pallas as pl
from jax.experimental.pallas import tpu as pltpu
from jax.sharding import Mesh
from jax.sharding import PartitionSpec as P

MESH = pl.DeviceIdType.MESH
F32, BF16 = jnp.float32, jnp.bfloat16
EPS = 1e-06
NX, NY = 4, 8
GROUPS, LANES8 = 16, 8
BLK = 256
STEP = 4


def kernel(
    acts_hbm, saved_hbm, grad_hbm, ga_hbm, gx_hbm, bias_a, bias_x, rate_param, gain, layers,
    acts_out, grad_out, sums_out,
    w, wsrc, wfull, xin, out_buf,
    x0, x1, inv, sq, ac, hl, st_a, st_r, st_i, st_s, st_rs, qp, bn, dy, dn,
    pre_a, pre_x, ends, par, gsum,
    lines, ey0, ey1, ey1a, ey2, eyg, exg, xsum,
    load_sem, w_send, w_recv, i_send, i_recv, e_send, e_recv, n_send, n_recv, g_send, g_recv, o_send, o_recv,
):
    s, mx, my = lax.axis_index("section"), lax.axis_index("tm_0"), lax.axis_index("tm_1")
    ns = lax.axis_size("section")
    chans = x0.shape[-1]
    heads = chans // BLK
    own = chans // NX
    mine = heads // NX
    pieces = chans // 128

    def xp(d):
        return lax.rem(mx + (d + NX), NX)

    def yp(d):
        return lax.rem(my + (d + NY), NY)

    def at_x(d):
        return (s, xp(d), my)

    def at_y(d):
        return (s, mx, yp(d))

    def section(step, d):
        return (lax.rem(s + (step + ns), ns), xp(d), my)

    def part(x):
        return pl.ds(pl.multiple_of(x * own, own), own)

    loads = [
        pltpu.make_async_copy(ga_hbm, wsrc.at[:, :, 0], load_sem.at[0]),
        pltpu.make_async_copy(gx_hbm, wsrc.at[:, :, 1], load_sem.at[1]),
        pltpu.make_async_copy(ga_hbm.at[:, mx], w.at[:, mx, my, 0], load_sem.at[2]),
        pltpu.make_async_copy(gx_hbm.at[:, mx], w.at[:, mx, my, 1], load_sem.at[3]),
    ]
    sources = (saved_hbm, acts_hbm, grad_hbm)
    loads += [
        pltpu.make_async_copy(ref.at[:, part(mx)], xin.at[k, :, part(mx)], load_sem.at[4 + k])
        for k, ref in enumerate(sources)
    ]
    for c in loads:
        c.start()

    around = [(a, b) for b in (0, 1, 7, 2, 6, 3, 5, 4) for a in (0, 1, 3, 2) if a or b]
    peers = [(s, xp(a), yp(b)) for a, b in around]
    peers += [section(step, d) for step in (1, -1) for d in range(NX)]
    barrier = pltpu.get_barrier_semaphore()
    for dev in peers:
        pl.semaphore_signal(barrier, inc=1, device_id=dev, device_id_type=MESH)
    pl.semaphore_wait(barrier, len(peers))

    sent = []

    def send(src, dst, sems, k, dev):
        c = pltpu.make_async_remote_copy(
            src_ref=src, dst_ref=dst, send_sem=sems[0].at[k], recv_sem=sems[1].at[k],
            device_id=dev, device_id_type=MESH,
        )
        c.start()
        sent.append(c)

    def arrived(slot, sems, k):
        pltpu.make_async_remote_copy(
            src_ref=slot, dst_ref=slot, send_sem=sems[0].at[k], recv_sem=sems[1].at[k],
            device_id=at_x(1), device_id_type=MESH,
        ).wait_recv()

    wsems, isems, esems = (w_send, w_recv), (i_send, i_recv), (e_send, e_recv)
    nsems, gsems, osems = (n_send, n_recv), (g_send, g_recv), (o_send, o_recv)

    def inputs_start(k):
        for d in (2, 1, 3):
            send(sources[k].at[:, part(xp(d))], xin.at[k, :, part(mx)], isems, 3 * k + d - 1, at_x(d))

    def inputs_wait(k):
        loads[4 + k].wait()
        for d in (1, 3, 2):
            arrived(xin.at[k, :, part(xp(-d))], isems, 3 * k + d - 1)

    near = [(a, b) for a, b in around if b in (0, 1, 2, NY - 1, NY - 2)]
    per_slot = len(near) + 4

    def weights_start(l):
        for n, (a, b) in enumerate(near):
            send(wsrc.at[l, xp(a)], w.at[l, mx, my], wsems, per_slot * l + n, (s, xp(a), yp(b)))

    def near_wait(l, places):
        for n, (a, b) in enumerate(near):
            if b in places:
                arrived(w.at[l, xp(-a), yp(-b)], wsems, per_slot * l + n)

    lo, hi = slice(0, NX // 2), slice(NX // 2, NX)

    def weights_pass(l):
        near_wait(l, (2, NY - 2))
        k = per_slot * l + len(near)
        for n, (xs, y, d) in enumerate(((lo, -2, 2), (hi, 2, -2), (slice(None), -2, 1), (slice(None), 2, -1))):
            ref = w.at[l, xs, yp(y)]
            send(ref, ref, wsems, k + n, at_y(d))

    def weights_wait(l):
        near_wait(l, (0, 1, NY - 1))
        k = per_slot * l + len(near)
        for n, (xs, y) in enumerate(((lo, 4), (hi, 4), (slice(None), -3), (slice(None), 3))):
            arrived(w.at[l, xs, yp(y)], wsems, k + n)

    class Exchange:
        def __init__(self, number, yb, sems=esems):
            self.base, self.yb, self.sems = number * (NY - 1), yb, sems

        def start(self):
            for d in (4, 3, 5, 2, 6, 1, 7):
                send(self.yb.at[my], self.yb.at[my], self.sems, self.base + d - 1, at_y(d))

        def wait(self):
            for d in range(1, NY):
                arrived(self.yb.at[yp(-d)], self.sems, self.base + d - 1)

    e0 = [Exchange(k, ey0.at[k]) for k in (0, 1)]
    e1 = Exchange(2, ey1)
    e1a = Exchange(3, ey1a)
    e2 = Exchange(4, ey2)
    eg = [Exchange(5 + l, eyg.at[l]) for l in (0, 1)]

    y = jnp.exp(rate_param[...])
    rate = y * (1.0 + y * (-1.0 / 2 + y * (1.0 / 3 + y * (-1.0 / 4 + y * (1.0 / 5 + y * (-1.0 / 6))))))
    par[0] = -8.0 * rate
    par[1] = y / (1.0 + y)
    live = [jnp.minimum(jnp.maximum(layers[0] - l, 0), 1).astype(F32) for l in (0, 1)]

    tok = lax.broadcasted_iota(jnp.int32, (128, 128), 1)
    row = lax.broadcasted_iota(jnp.int32, (128, 128), 0)
    to_runs = (tok == (row % LANES8) * GROUPS + row // LANES8).astype(F32).astype(BF16)
    to_tokens = (row == (tok % LANES8) * GROUPS + tok // LANES8).astype(F32).astype(BF16)
    sub = lax.broadcasted_iota(jnp.int32, (LANES8, chans), 0)
    sub16 = lax.broadcasted_iota(jnp.int32, (pieces, 128), 0)

    def cols_of(h):
        return pl.ds(pl.multiple_of(h * BLK, BLK), BLK)

    def over_heads(body, lo=0, hi=None):
        def step(h, _):
            body(h, cols_of(h))
            return 0

        lax.fori_loop(lo, heads if hi is None else hi, step, 0)

    def chunks():
        return [pl.ds(c * STEP, STEP) for c in range(GROUPS // STEP)]

    def runs3(v):
        return v.reshape(GROUPS, LANES8, v.shape[-1])

    def rows2(v):
        return v.reshape(GROUPS * LANES8, v.shape[-1])

    def squares(x):
        sq = x * x
        return sq[..., :128] + sq[..., 128:]

    def params_of(h):
        return pl.ds(pl.multiple_of((mx * mine + h) * BLK, BLK), BLK)

    def over_blocks(body):
        def step(b, _):
            for h in range(mine):
                body(b * mine + h, cols_of(b * mine + h), h, b)
            return 0

        lax.fori_loop(0, NX, step, 0)

    def share(n):
        tile = jnp.zeros((128, 128), F32)
        for b in range(NX):
            both = sq[mine * b]
            for k in range(1, mine):
                both += sq[mine * b + k]
            tile = jnp.where(tok == b, jnp.sum(rows2(both), axis=1, keepdims=True), tile)
        xsum[n, mx] = tile.T[:LANES8]
        for d in (2, 1, 3):
            send(xsum.at[n, mx], xsum.at[n, mx], nsems, 3 * n + d - 1, at_x(d))

    def shared(n):
        for d in (1, 3, 2):
            arrived(xsum.at[n, xp(-d)], nsems, 3 * n + d - 1)
        total = xsum[n, 0]
        for x in range(1, NX):
            total += xsum[n, x]
        return total * (1.0 / chans)

    def put_rows(slot, tile):
        turned = tile.T
        for b in range(NX):
            inv[slot, b] = runs3(jnp.broadcast_to(turned[:, b : b + 1], (128, BLK)))

    def put_inv(slot, n):
        put_rows(slot, lax.rsqrt(shared(n) + EPS))

    def permuted(k, dst, summed):
        def body(v, cols):
            x = runs3(jnp.dot(to_runs, xin[k, :, cols], preferred_element_type=F32))
            dst[:, :, cols] = x
            if summed:
                sq[v] = squares(x)

        over_heads(body)

    def assemble(l):
        for g in (0, 1):
            for k in range(mine):
                wfull[l, g, k] = w[l, :, :, g, k].astype(F32).reshape(BLK, BLK).astype(BF16)

    def sigmoid(v):
        return 1.0 / (1.0 + jnp.exp(-v))

    def forward(l, stream, xref, kk, sl):
        def body(v, cols, h, b):
            pc = params_of(h)
            g = gain[pl.ds(l, 1), pc]
            ba, bx = bias_a[pl.ds(l, 1), pc], bias_x[pl.ds(l, 1), pc]
            k8 = par[0, pl.ds(l, 1), pc]
            w_a, w_x = wfull[l, 0, h], wfull[l, 1, h]
            u = rows2(xref[:, :, cols] * inv[kk, b] * g).astype(BF16)
            pre_a[h] = runs3(jnp.dot(u, w_a, preferred_element_type=F32))
            pre_x[h] = runs3(jnp.dot(u, w_x, preferred_element_type=F32))
            cum_a = jnp.ones((LANES8, BLK), F32)
            cum_h = jnp.zeros((LANES8, BLK), F32)
            for c, rows in enumerate(chunks()):
                uf = (xref[rows, :, cols] * inv[kk, b, rows] * g).astype(BF16).astype(F32)
                r = sigmoid(pre_a[h, rows] + ba)
                i = sigmoid(pre_x[h, rows] + bx)
                log_a = r * k8
                a = jnp.exp(log_a)
                z = log_a * 2.0
                p = 1.0 / 120 + z * (1.0 / 720)
                p = 1.0 / 24 + z * p
                p = 1.0 / 6 + z * p
                p = 0.5 + z * p
                p = 1.0 + z * p
                sc2 = -(z * p)
                rs = lax.rsqrt(jnp.maximum(sc2, 1e-36))
                sc = sc2 * rs
                up = sc * i * uf
                if stream == 0:
                    st_a[l, rows, :, cols] = a
                    st_r[l, rows, :, cols] = r
                    st_i[l, rows, :, cols] = i
                    st_s[l, rows, :, cols] = sc
                    st_rs[l, rows, :, cols] = rs
                for t in range(STEP):
                    cum_a = cum_a * a[t]
                    cum_h = a[t] * cum_h + up[t]
                    ac[sl, c * STEP + t + 1, :, cols] = cum_a
                    hl[sl, c * STEP + t + 1, :, cols] = cum_h
            ac[sl, 0, :, cols] = jnp.ones((LANES8, BLK), F32)
            hl[sl, 0, :, cols] = jnp.zeros((LANES8, BLK), F32)

        over_blocks(body)

    def shifted(v, n, fill):
        if n > 0:
            return jnp.where(sub >= n, pltpu.roll(v, n, 0), fill)
        return jnp.where(sub < LANES8 + n, pltpu.roll(v, LANES8 + n, 0), fill)

    def joined(a, h, sign):
        for n in (1, 2, 4):
            h = a * shifted(h, sign * n, 0.0) + h
            a = a * shifted(a, sign * n, 1.0)
        return a, h

    def put_summary(dst, k, full, at):
        for g in range(pieces):
            lines[k, g : g + 1, :] = full[at : at + 1, 128 * g : 128 * (g + 1)]
        dst[my, k] = lines[k].astype(BF16)

    def summarise(sl, dst):
        a, h = joined(ac[sl, GROUPS], hl[sl, GROUPS], 1)
        ends[sl, 0] = shifted(a, 1, 1.0)
        ends[sl, 1] = shifted(h, 1, 0.0)
        put_summary(dst, 0, jnp.log(a), LANES8 - 1)
        put_summary(dst, 1, h, LANES8 - 1)

    def summarise_back(l, dst, k):
        a, z = joined(bn[l, GROUPS], qp[l, GROUPS], -1)
        ends[3 + l, 0] = shifted(a, -1, 1.0)
        ends[3 + l, 1] = shifted(z, -1, 0.0)
        put_summary(dst, k, z, 0)

    def read(y, k):
        vals = [y[t, k].astype(F32) for t in range(NY)]
        return [jnp.exp(v) for v in vals] if k == 0 else vals

    def entering(yb):
        ya, yh = read(yb, 0), read(yb, 1)
        a, h = ya[0], yh[0]
        for t in range(1, NY):
            h = ya[t] * h + yh[t]
            a = ya[t] * a
        per = pieces // NX
        state = jnp.zeros((pieces, 128), F32)
        for _ in range(NX - 1):
            state = jnp.where(sub16 >= per, pltpu.roll(a * state + h, per, 0), 0.0)
        for t in range(NY - 1):
            state = jnp.where(t < my, ya[t] * state + yh[t], state)
        return state

    def entering_back(first, second, kz):
        ya = read(first, 0)
        yz = [second[t, kz].astype(F32) for t in range(NY)]
        a, z = ya[NY - 1], yz[NY - 1]
        for t in reversed(range(NY - 1)):
            z = ya[t] * z + yz[t]
            a = ya[t] * a
        per = pieces // NX
        state = jnp.zeros((pieces, 128), F32)
        for _ in range(NX - 1):
            state = jnp.where(sub16 < pieces - per, pltpu.roll(a * state + z, pieces - per, 0), 0.0)
        for t in reversed(range(1, NY)):
            state = jnp.where(t > my, ya[t] * state + yz[t], state)
        return state

    def put_entering(k, h):
        for g in range(pieces):
            c = slice(128 * g, 128 * (g + 1))
            ends[k, 2, :, c] = ends[k, 1, :, c] + ends[k, 0, :, c] * h[g : g + 1]

    def next_layer(src, sl, dst):
        def body(v, cols):
            c = ends[sl, 2, :, cols]
            for k in range(GROUPS // STEP):
                rows, later = pl.ds(k * STEP, STEP), pl.ds(k * STEP + 1, STEP)
                st = hl[sl, later, :, cols] + ac[sl, later, :, cols] * c
                x = (src[rows, :, cols] + live[0] * st).astype(BF16).astype(F32)
                dst[rows, :, cols] = x
                sq[v, rows] = squares(x)

        over_heads(body)

    def last_layer(src, sl):
        def body(h, cols):
            c = ends[sl, 2, :, cols]
            st = hl[sl, pl.ds(1, GROUPS), :, cols] + ac[sl, pl.ds(1, GROUPS), :, cols] * c
            x = rows2(src[:, :, cols] + live[1] * st).astype(BF16)
            out_buf[0, :, cols] = jnp.dot(to_tokens, x, preferred_element_type=F32).astype(BF16)

        over_heads(body)

    def scan_back(l, cols):
        z = jnp.zeros((LANES8, BLK), F32)
        b = jnp.ones((LANES8, BLK), F32)
        for t in reversed(range(GROUPS)):
            q = live[l] * dy[t, :, cols] + z
            qp[l, t, :, cols] = q
            bn[l, t, :, cols] = b
            a = st_a[l, t, :, cols]
            z = a * q
            b = a * b
        qp[l, GROUPS, :, cols] = z
        bn[l, GROUPS, :, cols] = b

    def backward(l, xref):
        def body(v, cols, h, b):
            pc = params_of(h)
            g = gain[pl.ds(l, 1), pc]
            k8 = par[0, pl.ds(l, 1), pc]
            c, zin = ends[l, 2, :, cols], ends[3 + l, 2, :, cols]
            sums = [jnp.zeros((LANES8, BLK), F32) for _ in range(3)]
            for rows in chunks():
                q = qp[l, rows, :, cols] + bn[l, rows, :, cols] * zin
                a, r, i = st_a[l, rows, :, cols], st_r[l, rows, :, cols], st_i[l, rows, :, cols]
                sc, rs = st_s[l, rows, :, cols], st_rs[l, rows, :, cols]
                uf = (xref[rows, :, cols] * inv[l, b, rows] * g).astype(BF16).astype(F32)
                before = hl[l, rows, :, cols] + ac[l, rows, :, cols] * c
                iu = i * uf
                qs = q * sc
                d_log = q * a * (before - iu * a * rs)
                dr = d_log * r
                d_a = dr * k8 * (1.0 - r)
                d_x = qs * iu * (1.0 - i)
                sums[0] += jnp.sum(d_a, axis=0)
                sums[1] += jnp.sum(d_x, axis=0)
                sums[2] += jnp.sum(dr, axis=0)
                pre_a[h, rows] = d_a
                pre_x[h, rows] = d_x
                dn[rows, :, cols] = qs * i
            for k in range(3):
                gsum[l, k, :, cols] = sums[k]
            nt = (((1,), (1,)), ((), ()))
            mixed = lax.dot_general(rows2(pre_a[h]).astype(BF16), wfull[l, 0, h], nt, preferred_element_type=F32)
            mixed += lax.dot_general(rows2(pre_x[h]).astype(BF16), wfull[l, 1, h], nt, preferred_element_type=F32)
            pre_a[h] = runs3(mixed)
            total = jnp.zeros((LANES8, BLK), F32)
            for rows in chunks():
                n = xref[rows, :, cols] * inv[l, b, rows]
                du = dn[rows, :, cols] + pre_a[h, rows]
                dnn = du * n
                total += jnp.sum(dnn, axis=0)
                dn[rows, :, cols] = du * g
                t = dnn * g
                sq[v, rows] = t[..., :128] + t[..., 128:]
            gsum[l, 3, :, cols] = total

        over_blocks(body)

    def through_norm(l, xref, finish, lo=0, hi=None):
        def body(v, cols):
            b = v // mine
            for rows in chunks():
                n = xref[rows, :, cols] * inv[l, b, rows]
                dy[rows, :, cols] = dy[rows, :, cols] + inv[l, b, rows] * (dn[rows, :, cols] - n * inv[3, b, rows])
            finish(cols)

        over_heads(body, lo, hi)

    def send_sums(l):
        for k, source in enumerate((3, 0, 1, 2)):
            v = gsum[l, source, :, :own]
            for b in range(1, NX):
                v += gsum[l, source, :, b * own : (b + 1) * own]
            v = jnp.sum(v, axis=0, keepdims=True)
            if k == 3:
                v = v * (-8.0 * par[1, pl.ds(l, 1), part(mx)])
            for g in range(own // 128):
                at = k * (own // 128) + g
                eyg[l, my, at : at + 1, :] = v[:, 128 * g : 128 * (g + 1)]
        eg[l].start()

    def pass_sums(l):
        eg[l].wait()
        total = eyg[l, 0]
        for t in range(1, NY):
            total += eyg[l, t]
        exg[l, mx] = total
        for d in (2, 1, 3):
            send(exg.at[l, mx], exg.at[l, mx], gsems, 3 * l + d - 1, at_x(d))

    def put_sums(l):
        for d in (1, 3, 2):
            arrived(exg.at[l, xp(-d)], gsems, 3 * l + d - 1)
        sums_out[l] = exg[l]

    def deliver(k, result, step, d):
        send(out_buf.at[k, :, part(xp(d))], result.at[:, part(mx)], osems, NX * k + d, section(step, d))

    def delivered(k, result, d):
        arrived(result.at[:, part(xp(-d))], osems, NX * k + d)

    loads[0].wait()
    loads[1].wait()
    inputs_start(0)
    weights_start(0)
    inputs_wait(0)
    permuted(0, x0.at[0], True)
    share(0)
    weights_pass(0)
    weights_start(1)
    inputs_start(1)
    inputs_start(2)
    put_inv(0, 0)
    loads[2].wait()
    loads[3].wait()
    weights_wait(0)
    assemble(0)
    forward(0, 0, x0.at[0], 0, 0)
    summarise(0, ey0.at[0])
    e0[0].start()
    inputs_wait(1)
    permuted(1, x0.at[1], True)
    share(1)
    weights_pass(1)
    inputs_wait(2)
    permuted(2, dy, False)
    e0[0].wait()
    put_entering(0, entering(ey0.at[0]))
    next_layer(x0.at[0], 0, x1.at[0])
    share(2)
    put_inv(2, 1)
    forward(0, 1, x0.at[1], 2, 2)
    summarise(2, ey0.at[1])
    e0[1].start()
    weights_wait(1)
    assemble(1)
    put_inv(1, 2)
    forward(1, 0, x1.at[0], 1, 1)
    over_heads(lambda v, cols: scan_back(1, cols))
    summarise(1, ey1)
    summarise_back(1, ey1, 2)
    e1.start()
    e0[1].wait()
    put_entering(2, entering(ey0.at[1]))
    next_layer(x0.at[1], 2, x1.at[1])
    share(3)
    e1.wait()
    put_entering(1, entering(ey1))
    put_entering(4, entering_back(ey1, ey1, 2))
    backward(1, x1.at[0])
    share(4)
    put_inv(2, 3)
    forward(1, 1, x1.at[1], 2, 2)
    put_rows(3, shared(4))
    through_norm(1, x1.at[0], lambda cols: scan_back(0, cols))
    summarise_back(0, ey2, 0)
    e2.start()
    summarise(2, ey1a)
    e1a.start()
    send_sums(1)
    e2.wait()
    put_entering(3, entering_back(ey0.at[0], ey2, 0))
    backward(0, x0.at[0])
    share(5)
    send_sums(0)
    e1a.wait()
    put_entering(2, entering(ey1a))
    last_layer(x1.at[1], 2)
    for d in (2, 1, 3, 0):
        deliver(0, acts_out, 1, d)
    pass_sums(1)
    put_rows(3, shared(5))

    def finish(cols):
        out_buf[1, :, cols] = jnp.dot(to_tokens, rows2(dy[:, :, cols]).astype(BF16), preferred_element_type=F32).astype(BF16)

    for d in (2, 1, 3, 0):
        through_norm(0, x0.at[0], finish, mine * xp(d), mine * xp(d) + mine)
        deliver(1, grad_out, -1, d)
    pass_sums(0)
    put_sums(1)
    put_sums(0)
    for d in range(NX):
        delivered(0, acts_out, d)
        delivered(1, grad_out, d)
    for c in sent:
        c.wait_send()


def hand_over(acts, grad, sums, acts_out, grad_out, o_gain, o_ba, o_bx, o_rate):
    acts_out[...] = acts[...]
    grad_out[...] = grad[...]
    per = sums.shape[2] // 4
    for k, ref in enumerate((o_gain, o_ba, o_bx, o_rate)):
        for g in range(ref.shape[-1] // 128):
            ref[:, 128 * g : 128 * (g + 1)] = sums[:, g // per, k * per + g % per, :]


def local(acts_in, saved_in, grad_in, gate_a, gate_x, bias_a, bias_x, rate_param, norm_gain, section_layers):
    _, tokens, chans = acts_in.shape
    slots, heads = gate_a.shape[1:3]
    full = (GROUPS, LANES8, chans)
    vec = (chans // 128, 128)
    sem = pltpu.SemaphoreType.DMA
    any_spec = pl.BlockSpec(memory_space=pl.ANY)
    vmem_spec = pl.BlockSpec(memory_space=pltpu.VMEM)
    mine = heads // NX
    vm = pltpu.VMEM
    outs = pl.pallas_call(
        kernel,
        out_shape=[jax.ShapeDtypeStruct((tokens, chans), BF16)] * 2
        + [jax.ShapeDtypeStruct((slots, NX, *vec), F32)],
        in_specs=[any_spec] * 5 + [vmem_spec] * 4 + [pl.BlockSpec(memory_space=pltpu.SMEM)],
        out_specs=[any_spec] * 2 + [vmem_spec],
        scratch_shapes=[
            vm((slots, NX, NY, 2, mine, 8, BLK), BF16),
            vm((slots, NX, 2, mine, 8, BLK), BF16),
            vm((slots, 2, mine, BLK, BLK), BF16),
            vm((3, tokens, chans), BF16),
            vm((2, tokens, chans), BF16),
            vm((2, *full), F32),
            vm((2, *full), F32),
            vm((4, NX, GROUPS, LANES8, BLK), F32),
            vm((heads, GROUPS, LANES8, 128), F32),
            vm((3, GROUPS + 1, LANES8, chans), F32),
            vm((3, GROUPS + 1, LANES8, chans), F32),
            vm((slots, *full), F32),
            vm((slots, *full), F32),
            vm((slots, *full), F32),
            vm((slots, *full), F32),
            vm((slots, *full), F32),
            vm((slots, GROUPS + 1, LANES8, chans), F32),
            vm((slots, GROUPS + 1, LANES8, chans), F32),
            vm(full, F32),
            vm(full, F32),
            vm((mine, GROUPS, LANES8, BLK), F32),
            vm((mine, GROUPS, LANES8, BLK), F32),
            vm((5, 3, LANES8, chans), F32),
            vm((2, slots, chans), F32),
            vm((slots, 4, LANES8, chans), F32),
            vm((3, *vec), F32),
            vm((2, NY, 2, *vec), BF16),
            vm((NY, 3, *vec), BF16),
            vm((NY, 2, *vec), BF16),
            vm((NY, 1, *vec), BF16),
            vm((slots, NY, *vec), F32),
            vm((slots, NX, *vec), F32),
            vm((6, NX, LANES8, 128), F32),
            sem((7,)),
            *[sem((slots * (5 * NX - 1 + 4),))] * 2,
            *[sem((3 * (NX - 1),))] * 2,
            *[sem((7 * (NY - 1),))] * 2,
            *[sem((6 * (NX - 1),))] * 2,
            *[sem((slots * (NX - 1),))] * 2,
            *[sem((2 * NX,))] * 2,
        ],
        compiler_params=pltpu.CompilerParams(
            collective_id=0, has_side_effects=True, vmem_limit_bytes=60 * 1024 * 1024
        ),
    )(
        acts_in[0], saved_in[0], grad_in[0],
        *(g[0].reshape(slots, NX, mine, 8, BLK) for g in (gate_a, gate_x)),
        bias_a[0], bias_x[0], rate_param[0], norm_gain[0], section_layers,
    )
    outs = pl.pallas_call(
        hand_over,
        out_shape=[jax.ShapeDtypeStruct((tokens, chans), BF16)] * 2
        + [jax.ShapeDtypeStruct((slots, chans), F32)] * 4,
        in_specs=[vmem_spec] * 3,
        out_specs=[vmem_spec] * 6,
    )(*outs)
    return tuple(o[None] for o in outs)


def solution(mesh):
    finer = Mesh(mesh.devices.reshape(mesh.shape["section"], NX, NY), ("section", "tm_0", "tm_1"))
    tm = ("tm_0", "tm_1")
    act = P("section", tm, None)
    gate = P("section", None, None, tm, None)
    small = P("section", None, None)
    return jax.shard_map(
        local,
        mesh=finer,
        in_specs=(act, act, act, gate, gate, small, small, small, small, P("section")),
        out_specs=(act, act, small, small, small, small),
        check_vma=False,
    )
```
